32 devices in a mesh: beam: 2 (over x), freq: 16 (over z, y, core).
Axes of the slice: x: 2, y: 2, z: 4, core: 2. Of those that a mesh axis runs over, the one named last changes fastest.
Arguments:
- spectrum: bfloat16 [2, 65536], P(None, ('beam', 'freq')), parts along dimension 1, may hold values from -6 to 6
- template_bank: bfloat16 [2, 256, 1024], replicated, may hold values from -0.125 to 0.125
- template_index: int32 [128], replicated, may hold values from 0 to 255
Outputs:
- harmonic_sum: float32 [128, 65536], P(None, ('beam', 'freq')), parts along dimension 1
The draws below stay inside these ranges and needn't reach their ends.
There are 2 independent parts, one for each index of `beam`. The reference program is written for one: setup_inputs(seed, part) draws one part's arguments, and reference() takes and returns one part's arrays. A program takes and returns all parts, laid end to end along the dimension named above; an argument that names none is the same for every part. Nothing has to cross between parts.
Inputs may be any that keep to these rules, and one draw needn't show every extreme that they name: `template_index`: entry z names the bank template of acceleration row z.
All inputs are finite; a program needn't handle non-finite values.
Results may differ from the reference program's by a relative error of at most 0.002.
Values may be sent and summed in bfloat16 or wider, within the bound.
No kernel may reach another device: no remote copies, remote signals or barrier semaphores. Data moves between devices by JAX's collectives and lax.ppermute only.
A program may use at most 64 MiB of HBM per device.

```python
import jax
import jax.numpy as jnp
from jax import lax

ZROWS = 128
TAPS = 1024
NBANK = 256
BINS = 32768


def set_ends(array, stream_key, smallest, largest):
    shape = array.shape
    spot = [jax.random.randint(jax.random.fold_in(stream_key, axis), (), 0, shape[axis]) for axis in range(len(shape))]
    array = array.at[tuple(spot)].set(smallest)
    longest = shape.index(max(shape))
    spot[longest] = (spot[longest] + 1) % shape[longest]
    return array.at[tuple(spot)].set(largest)


def shard_levels(rng, shape, pieces, low, high):
    factor_of, own = 1.0, jax.random.fold_in(rng, 6)
    for dim, shards_of in pieces:
        draws = jnp.exp(jax.random.uniform(jax.random.fold_in(own, dim), (shards_of,), jnp.float32, low / len(pieces), high / len(pieces)))
        factor_of = factor_of * jnp.repeat(draws, shape[dim] // shards_of).reshape([-1 if axis == dim else 1 for axis in range(len(shape))])
    return factor_of


def bell_draw(stream_key, shape, spread, limit, cuts=(), kind=jnp.bfloat16):
    values = spread * jax.random.normal(stream_key, shape, jnp.float32)
    if cuts:
        values = values * shard_levels(stream_key, shape, cuts, -0.22, 0.18)
    return jnp.clip(values, -limit, limit).astype(kind)


def setup_inputs(seed: int = 0, part: int = 0) -> dict:
    key_of = jax.random.split(jax.random.key(seed), 4)
    part_splits = jax.random.split(jax.random.fold_in(key_of[3], part), 4)
    return {
        "spectrum": bell_draw(part_splits[0], (2, BINS), 1.0, 6.0, ((1, 16),)),
        "template_bank": bell_draw(key_of[1], (2, NBANK, TAPS), (2 * TAPS) ** -0.5, 0.125),
        "template_index": set_ends(jax.random.randint(key_of[2], (ZROWS,), 0, NBANK), jax.random.fold_in(key_of[2], 1), 0, NBANK - 1).astype(jnp.int32),
    }


def reference(spectrum, template_bank, template_index):
    half_taps = TAPS // 2
    length_fft = 2 * BINS
    template_re = template_bank[0][template_index].astype(jnp.float32)
    template_im = template_bank[1][template_index].astype(jnp.float32)
    signal = lax.complex(spectrum[0].astype(jnp.float32), spectrum[1].astype(jnp.float32))
    padded = jnp.pad(signal, (half_taps, length_fft - BINS - half_taps))
    signal_freq = jnp.fft.fft(padded)

    def correlate_row(pair):
        row_re, row_im = pair
        row = lax.complex(row_re, row_im)
        row_pad = jnp.pad(row, (0, length_fft - TAPS))
        kernel_freq = jnp.conj(jnp.fft.fft(jnp.conj(row_pad)))
        correlated = jnp.fft.ifft(signal_freq * kernel_freq)[:BINS]
        real_part = jnp.real(correlated)
        imag_part = jnp.imag(correlated)
        return (real_part * real_part + imag_part * imag_part).astype(jnp.bfloat16)

    plane = lax.map(correlate_row, (template_re, template_im))
    total = plane.astype(jnp.float32)
    for numerator, denominator in ((1, 2), (1, 4), (3, 4)):
        row_index = (jnp.arange(ZROWS, dtype=jnp.int32) * numerator) // denominator
        col_index = (jnp.arange(BINS, dtype=jnp.int32) * numerator) // denominator
        total = total + plane[row_index][:, col_index].astype(jnp.float32)
    return total
```

```python
import functools

import jax
import jax.numpy as jnp
from jax import lax
from jax.experimental import pallas as pl
from jax.experimental.pallas import tpu as pltpu
from jax.sharding import PartitionSpec as P

LANES = 128
HARMONICS = ((3, 4), (1, 2), (1, 4))
F32 = jnp.float32
BF16 = jnp.bfloat16


def iota(shape, dim):
    return lax.broadcasted_iota(jnp.int32, shape, dim)


def weights_kernel(index_ref, bank_ref, w_ref):
    rows = index_ref.shape[1]
    bank = bank_ref.shape[1]
    taps = bank_ref.shape[2]
    picked = (iota((bank, rows), 0) == index_ref[...]).astype(BF16)
    order = iota((LANES, LANES), 1)
    order = (order // 8) * 8 + 7 - order % 8
    flip = (iota((LANES, LANES), 0) == order).astype(BF16)
    for m in range(taps // LANES):
        part = []
        for c in range(2):
            chunk = bank_ref[c, :, m * LANES : (m + 1) * LANES]
            chunk = jnp.dot(chunk, flip, preferred_element_type=F32).astype(BF16)
            part.append(
                lax.dot_general(
                    picked, chunk, (((0,), (0,)), ((), ())), preferred_element_type=F32
                )
            )
        re, im = part
        w_ref[m, :rows, :LANES] = re.astype(BF16)
        w_ref[m, :rows, LANES:] = (-im).astype(BF16)
        w_ref[m, rows:, :LANES] = im.astype(BF16)
        w_ref[m, rows:, LANES:] = re.astype(BF16)


def hankel(window, h_ref):
    length = window.shape[1]
    kept = length - LANES
    for c in range(2):
        row = jnp.broadcast_to(window[c : c + 1, :], (8, length))
        for a in range(0, LANES // 8, 2):
            pair = [
                pltpu.roll(row, length - 8 * k - 7, 1, stride=1, stride_axis=0)[:, :kept]
                for k in (a, a + 1)
            ]
            at = c * LANES + 8 * a
            h_ref[at : at + 16, :kept] = jnp.concatenate(pair, 0).astype(BF16)


def power(w_ref, h_ref, rows, col, width):
    all_rows = w_ref.shape[1] // 2
    count = w_ref.shape[0]
    right = jnp.concatenate(
        [h_ref[:, col + m * LANES : col + m * LANES + width] for m in range(count)], 0
    )
    parts = []
    for start in (0, all_rows):
        left = jnp.concatenate([w_ref[m, start : start + rows, :] for m in range(count)], 1)
        parts.append(jnp.dot(left, right, preferred_element_type=F32))
    re, im = parts
    return (re * re + im * im).astype(BF16)


def plane_kernel(w_ref, all_ref, out_ref, line_ref, h_ref, own_ref, *planes):
    owners, _, block = all_ref.shape
    rows = out_ref.shape[0]
    taps = w_ref.shape[0] * LANES
    half = taps // 2
    device = lax.axis_index("freq")
    line_ref[:, :half] = jnp.zeros((2, half), F32)
    line_ref[:, half + owners * block :] = jnp.zeros((2, half), F32)
    for j in range(owners):
        line_ref[:, half + j * block : half + (j + 1) * block] = all_ref[j].astype(F32)
    tile = 256
    pieces = []
    for (num, den), plane_ref in zip(HARMONICS + ((1, 1),), planes + (own_ref,)):
        part_rows, part_cols = plane_ref.shape
        start = pl.multiple_of(device * part_cols, LANES)
        hankel(line_ref[:, pl.ds(start, part_cols + taps)], h_ref)
        for col in range(0, part_cols, tile):
            plane_ref[:, col : col + tile] = power(w_ref, h_ref, part_rows, col, tile)
        if den == 1:
            continue
        group = LANES * num
        wide = LANES * den
        groups = part_cols // group
        expand = (
            iota((group, wide), 1) * num // den == iota((group, wide), 0)
        ).astype(BF16)
        stacked = jnp.concatenate(
            [plane_ref[:, g * group : (g + 1) * group] for g in range(groups)], 0
        )
        spread = jnp.dot(stacked, expand, preferred_element_type=F32).astype(BF16)
        pieces.append(
            jnp.concatenate(
                [spread[g * part_rows : (g + 1) * part_rows] for g in range(groups)], 1
            )
        )
    picks = [
        (iota((rows, p.shape[0]), 0) * num // den == iota((rows, p.shape[0]), 1)).astype(BF16)
        for (num, den), p in zip(HARMONICS, pieces)
    ]
    total = jnp.dot(
        jnp.concatenate(picks, 1), jnp.concatenate(pieces, 0), preferred_element_type=F32
    )
    out_ref[...] = own_ref[...].astype(F32) + total


def body(spectrum, template_bank, template_index):
    owners = lax.axis_size("freq")
    block = spectrum.shape[1]
    rows = template_index.shape[0]
    taps = template_bank.shape[2]
    vmem = pl.BlockSpec(memory_space=pltpu.VMEM)
    weights = pl.pallas_call(
        weights_kernel,
        out_shape=jax.ShapeDtypeStruct((taps // LANES, 2 * rows, 2 * LANES), BF16),
        in_specs=[vmem] * 2,
        out_specs=vmem,
        compiler_params=pltpu.CompilerParams(vmem_limit_bytes=32 << 20),
    )(template_index.reshape(1, rows), template_bank)
    everything = lax.all_to_all(
        jnp.broadcast_to(spectrum, (owners, 2, block)), "freq", split_axis=0, concat_axis=0, tiled=True
    )
    return pl.pallas_call(
        plane_kernel,
        out_shape=jax.ShapeDtypeStruct((rows, block), F32),
        in_specs=[vmem] * 2,
        out_specs=vmem,
        scratch_shapes=[
            pltpu.VMEM((2, owners * block + taps), F32),
            pltpu.VMEM((2 * LANES, block + taps - LANES), BF16),
            pltpu.VMEM((rows, block), BF16),
        ]
        + [
            pltpu.VMEM((rows * num // den, block * num // den), BF16) for num, den in HARMONICS
        ],
        compiler_params=pltpu.CompilerParams(vmem_limit_bytes=48 << 20),
    )(weights, everything)


def solution(mesh):
    return jax.shard_map(
        body,
        mesh=mesh,
        in_specs=(P(None, ("beam", "freq")), P(), P()),
        out_specs=P(None, ("beam", "freq")),
        check_vma=False,
    )
```

```python
import jax
import jax.numpy as jnp
from jax import lax
from jax.experimental import pallas as pl
from jax.experimental.pallas import tpu as pltpu
from jax.sharding import PartitionSpec as P

LANES = 128
TILE = 256
HARMONICS = ((3, 4), (1, 2), (1, 4))
F32 = jnp.float32
BF16 = jnp.bfloat16
VMEM = pl.BlockSpec(memory_space=pltpu.VMEM)


def iota(shape, dim):
    return lax.broadcasted_iota(jnp.int32, shape, dim)


def dot(left, right):
    return jnp.dot(left, right, preferred_element_type=F32)


def square(pair):
    rows = pair.shape[0] // 2
    re, im = pair[:rows], pair[rows:]
    return (re * re + im * im).astype(BF16)


def hankel(window, h_ref):
    length = window.shape[1]
    kept = length - LANES
    for c in range(2):
        row = jnp.broadcast_to(window[c : c + 1, :], (8, length))
        for a in range(0, LANES // 8, 2):
            pair = [
                pltpu.roll(row, length - 8 * k - 7, 1, stride=1, stride_axis=0)[:, :kept]
                for k in (a, a + 1)
            ]
            at = c * LANES + 8 * a
            h_ref[at : at + 16, :kept] = jnp.concatenate(pair, 0).astype(BF16)


def hankel_tile(h_ref, col, steps, width=TILE):
    return jnp.concatenate(
        [h_ref[:, col + m * LANES : col + m * LANES + width] for m in steps], 0
    )


def weights(w_ref, steps, rows=None):
    all_rows = w_ref.shape[1] // 2
    if rows is None:
        return jnp.concatenate([w_ref[m] for m in steps], 1)
    return jnp.concatenate(
        [
            jnp.concatenate([w_ref[m, :rows], w_ref[m, all_rows : all_rows + rows]], 0)
            for m in steps
        ],
        1,
    )


def share_kernel(own_ref, shared_ref):
    for j in range(shared_ref.shape[0]):
        shared_ref[j] = own_ref[...]


def local_kernel(index_ref, bank_ref, own_ref, w_ref, inner_ref, edge_ref, h_ref):
    rows = index_ref.shape[1]
    bank = bank_ref.shape[1]
    taps = bank_ref.shape[2]
    half = taps // 2
    block = own_ref.shape[1]
    picked = (iota((bank, rows), 0) == index_ref[...]).astype(BF16)
    order = iota((LANES, LANES), 1)
    order = (order // 8) * 8 + 7 - order % 8
    flip = (iota((LANES, LANES), 0) == order).astype(BF16)
    count = taps // LANES
    for m in range(count):
        part = []
        for c in range(2):
            chunk = bank_ref[c, :, m * LANES : (m + 1) * LANES]
            chunk = dot(chunk, flip).astype(BF16)
            part.append(
                lax.dot_general(
                    picked, chunk, (((0,), (0,)), ((), ())), preferred_element_type=F32
                )
            )
        re, im = part
        w_ref[m, :rows, :LANES] = re.astype(BF16)
        w_ref[m, :rows, LANES:] = (-im).astype(BF16)
        w_ref[m, rows:, :LANES] = im.astype(BF16)
        w_ref[m, rows:, LANES:] = re.astype(BF16)
    zeros = jnp.zeros((2, half), F32)
    hankel(jnp.concatenate([zeros, own_ref[...].astype(F32), zeros], 1), h_ref)
    for col in range(0, block, TILE):
        steps = [
            m
            for m in range(count)
            if col + m * LANES + TILE + LANES - 1 > half and col + m * LANES < half + block
        ]
        got = dot(weights(w_ref, steps), hankel_tile(h_ref, col, steps))
        if half <= col < block - half:
            inner_ref[:, col - half : col - half + TILE] = square(got)
        else:
            at = col if col < half else col - block + 2 * half
            edge_ref[:, at : at + TILE] = got


def packed(w_ref, h_ref, rows, cols, pack):
    count = w_ref.shape[0]
    all_rows = w_ref.shape[1] // 2
    long = cols + (pack - 1) * LANES
    tiles = []
    left = jnp.concatenate(
        [
            jnp.concatenate(
                [w_ref[m + k, base : base + rows] for k in range(pack) for base in (0, all_rows)],
                0,
            )
            for m in range(0, count, pack)
        ],
        1,
    )
    col = 0
    while col < long:
        width = min(TILE, long - col)
        tiles.append(dot(left, hankel_tile(h_ref, col, range(0, count, pack), width)))
        col += width
    got = jnp.concatenate(tiles, 1)
    total = got[: 2 * rows, :cols]
    for k in range(1, pack):
        total = total + got[2 * rows * k : 2 * rows * (k + 1), k * LANES : k * LANES + cols]
    return square(total)


def plane_kernel(w_ref, inner_ref, edge_ref, all_ref, out_ref, line_ref, h_ref, side_ref, buffer_ref, sems):
    owners, _, block = all_ref.shape
    rows = w_ref.shape[1] // 2
    count = w_ref.shape[0]
    taps = count * LANES
    half = taps // 2
    device = lax.axis_index("freq")
    line_ref[:, :half] = jnp.zeros((2, half), F32)
    line_ref[:, half + owners * block :] = jnp.zeros((2, half), F32)
    for j in range(owners):
        line_ref[:, half + j * block : half + (j + 1) * block] = all_ref[j].astype(F32)

    pieces = []
    for num, den in HARMONICS:
        part_rows, part_cols = rows * num // den, block * num // den
        start = pl.multiple_of(device * part_cols, LANES)
        hankel(line_ref[:, pl.ds(start, part_cols + taps)], h_ref)
        pack = rows // part_rows
        if pack > 1:
            plane = packed(w_ref, h_ref, part_rows, part_cols, pack)
        else:
            left = weights(w_ref, range(count), part_rows)
            plane = jnp.concatenate(
                [
                    square(dot(left, hankel_tile(h_ref, col, range(count))))
                    for col in range(0, part_cols, TILE)
                ],
                1,
            )
        group = LANES * num
        wide = LANES * den
        groups = part_cols // group
        expand = (
            iota((group, wide), 1) * num // den == iota((group, wide), 0)
        ).astype(BF16)
        stacked = jnp.concatenate(
            [plane[:, g * group : (g + 1) * group] for g in range(groups)], 0
        )
        spread = dot(stacked, expand).astype(BF16)
        pieces.append(
            jnp.concatenate(
                [spread[g * part_rows : (g + 1) * part_rows] for g in range(groups)], 1
            )
        )

    own = pl.multiple_of(device * block, LANES)
    edges = []
    pad = jnp.zeros((2, 2 * LANES), F32)
    hankel(jnp.concatenate([line_ref[:, pl.ds(own, half)], pad], 1), side_ref)
    for col in range(0, half, TILE):
        steps = [m for m in range(count) if col + m * LANES < half]
        edges.append(edge_ref[:, col : col + TILE] + dot(weights(w_ref, steps), hankel_tile(side_ref, col, steps)))
    after = pl.multiple_of(own + half + block, LANES)
    hankel(jnp.concatenate([pad, line_ref[:, pl.ds(after, half)], pad[:, :LANES]], 1), side_ref)
    for col in range(0, half, TILE):
        steps = [m for m in range(count) if col + m * LANES >= 2 * half - 2 * LANES]
        shift = 2 * half - 2 * LANES
        edges.append(
            edge_ref[:, half + col : half + col + TILE]
            + dot(weights(w_ref, steps), hankel_tile(side_ref, col - shift, steps))
        )
    edges = [square(edge) for edge in edges]
    middle = len(edges) // 2
    own_plane = jnp.concatenate(edges[:middle] + [inner_ref[...]] + edges[middle:], 1)

    picks = jnp.concatenate(
        [
            (iota((rows, p.shape[0]), 0) * num // den == iota((rows, p.shape[0]), 1)).astype(BF16)
            for (num, den), p in zip(HARMONICS, pieces)
        ],
        1,
    )
    chunks = sems.shape[0]
    width = block // chunks
    copies = []
    for n in range(chunks):
        at = slice(n * width, (n + 1) * width)
        total = dot(picks, jnp.concatenate([p[:, at] for p in pieces], 0))
        buffer_ref[:, at] = own_plane[:, at].astype(F32) + total
        copy = pltpu.make_async_copy(buffer_ref.at[:, at], out_ref.at[:, at], sems.at[n])
        copy.start()
        copies.append(copy)
    for copy in copies:
        copy.wait()


def body(spectrum, template_bank, template_index):
    owners = lax.axis_size("freq")
    block = spectrum.shape[1]
    rows = template_index.shape[0]
    taps = template_bank.shape[2]
    half = taps // 2
    shared = pl.pallas_call(
        share_kernel,
        out_shape=jax.ShapeDtypeStruct((owners, 2, block), BF16),
        in_specs=[VMEM],
        out_specs=VMEM,
        name="share",
    )(spectrum)
    everything = lax.all_to_all(shared, "freq", split_axis=0, concat_axis=0, tiled=True)
    w, inner, edge = pl.pallas_call(
        local_kernel,
        out_shape=(
            jax.ShapeDtypeStruct((taps // LANES, 2 * rows, 2 * LANES), BF16),
            jax.ShapeDtypeStruct((rows, block - 2 * half), BF16),
            jax.ShapeDtypeStruct((2 * rows, 2 * half), F32),
        ),
        in_specs=[VMEM] * 3,
        out_specs=(VMEM,) * 3,
        scratch_shapes=[pltpu.VMEM((2 * LANES, block + taps - LANES), BF16)],
        compiler_params=pltpu.CompilerParams(vmem_limit_bytes=24 << 20),
        name="local",
    )(template_index.reshape(1, rows), template_bank, spectrum)
    return pl.pallas_call(
        plane_kernel,
        out_shape=jax.ShapeDtypeStruct((rows, block), F32),
        in_specs=[VMEM] * 4,
        out_specs=pl.BlockSpec(memory_space=pl.ANY),
        scratch_shapes=[
            pltpu.VMEM((2, owners * block + taps), F32),
            pltpu.VMEM((2 * LANES, block + taps - LANES), BF16),
            pltpu.VMEM((2 * LANES, half + LANES + TILE), BF16),
            pltpu.VMEM((rows, block), F32),
            pltpu.SemaphoreType.DMA((4,)),
        ],
        compiler_params=pltpu.CompilerParams(vmem_limit_bytes=32 << 20),
        name="plane",
    )(w, inner, edge, everything)


def solution(mesh):
    return jax.shard_map(
        body,
        mesh=mesh,
        in_specs=(P(None, ("beam", "freq")), P(), P()),
        out_specs=P(None, ("beam", "freq")),
        check_vma=False,
    )
```

```python
import jax
import jax.numpy as jnp
from jax import lax
from jax.experimental import pallas as pl
from jax.experimental.pallas import tpu as pltpu
from jax.sharding import PartitionSpec as P

LANES = 128
TILE = 256
HARMONICS = ((3, 4), (1, 2), (1, 4))
F32 = jnp.float32
BF16 = jnp.bfloat16
VMEM = pl.BlockSpec(memory_space=pltpu.VMEM)
ANY = pl.BlockSpec(memory_space=pl.ANY)
HBM = pl.BlockSpec(memory_space=pltpu.HBM)


def iota(shape, dim):
    return lax.broadcasted_iota(jnp.int32, shape, dim)


def dot(left, right):
    return jnp.dot(left, right, preferred_element_type=F32)


def square(pair):
    rows = pair.shape[0] // 2
    re, im = pair[:rows], pair[rows:]
    return (re * re + im * im).astype(BF16)


def hankel(window, h_ref):
    length = window.shape[1]
    kept = length - LANES
    for c in range(2):
        row = jnp.broadcast_to(window[c : c + 1, :], (8, length))
        for a in range(0, LANES // 8, 2):
            pair = [
                pltpu.roll(row, length - 8 * k - 7, 1, stride=1, stride_axis=0)[:, :kept]
                for k in (a, a + 1)
            ]
            at = c * LANES + 8 * a
            h_ref[at : at + 16, :kept] = jnp.concatenate(pair, 0).astype(BF16)


def hankel_tile(h_ref, col, steps, width=TILE):
    return jnp.concatenate(
        [h_ref[:, col + m * LANES : col + m * LANES + width] for m in steps], 0
    )


def weights(w_ref, steps, rows=None):
    all_rows = w_ref.shape[1] // 2
    if rows is None:
        return jnp.concatenate([w_ref[m] for m in steps], 1)
    return jnp.concatenate(
        [
            jnp.concatenate([w_ref[m, :rows], w_ref[m, all_rows : all_rows + rows]], 0)
            for m in steps
        ],
        1,
    )


def share_kernel(own_ref, shared_ref):
    for j in range(shared_ref.shape[0]):
        shared_ref[j] = own_ref[...]


def local_kernel(index_hbm, bank_hbm, own_hbm, w_ref, inner_ref, edge_ref, index_ref, bank_ref, own_ref, h_ref, sems):
    rows = index_ref.shape[1]
    bank = bank_ref.shape[1]
    taps = bank_ref.shape[2]
    half = taps // 2
    block = own_ref.shape[1]
    count = taps // LANES
    arrays = ((own_hbm, own_ref), (index_hbm, index_ref), (bank_hbm, bank_ref))
    copies = [pltpu.make_async_copy(*pair, sems.at[n]) for n, pair in enumerate(arrays)]
    for copy in copies:
        copy.start()
    order = iota((LANES, LANES), 1)
    order = (order // 8) * 8 + 7 - order % 8
    flip = (iota((LANES, LANES), 0) == order).astype(BF16)
    copies[0].wait()
    zeros = jnp.zeros((2, half), F32)
    hankel(jnp.concatenate([zeros, own_ref[...].astype(F32), zeros], 1), h_ref)
    copies[1].wait()
    picked = (iota((bank, rows), 0) == index_ref[...]).astype(BF16)
    copies[2].wait()
    for m in range(count):
        part = []
        for c in range(2):
            chunk = bank_ref[c, :, m * LANES : (m + 1) * LANES]
            chunk = dot(chunk, flip).astype(BF16)
            part.append(
                lax.dot_general(
                    picked, chunk, (((0,), (0,)), ((), ())), preferred_element_type=F32
                )
            )
        re, im = part
        w_ref[m, :rows, :LANES] = re.astype(BF16)
        w_ref[m, :rows, LANES:] = (-im).astype(BF16)
        w_ref[m, rows:, :LANES] = im.astype(BF16)
        w_ref[m, rows:, LANES:] = re.astype(BF16)
    for col in range(0, block, TILE):
        steps = [
            m
            for m in range(count)
            if col + m * LANES + TILE + LANES - 1 > half and col + m * LANES < half + block
        ]
        got = dot(weights(w_ref, steps), hankel_tile(h_ref, col, steps))
        if half <= col < block - half:
            inner_ref[:, col - half : col - half + TILE] = square(got)
        else:
            at = col if col < half else col - block + 2 * half
            edge_ref[:, at : at + TILE] = got


def packed(w_ref, h_ref, rows, cols, pack):
    count = w_ref.shape[0]
    all_rows = w_ref.shape[1] // 2
    long = cols + (pack - 1) * LANES
    tiles = []
    left = jnp.concatenate(
        [
            jnp.concatenate(
                [w_ref[m + k, base : base + rows] for k in range(pack) for base in (0, all_rows)],
                0,
            )
            for m in range(0, count, pack)
        ],
        1,
    )
    col = 0
    while col < long:
        width = min(TILE, long - col)
        tiles.append(dot(left, hankel_tile(h_ref, col, range(0, count, pack), width)))
        col += width
    got = jnp.concatenate(tiles, 1)
    total = got[: 2 * rows, :cols]
    for k in range(1, pack):
        total = total + got[2 * rows * k : 2 * rows * (k + 1), k * LANES : k * LANES + cols]
    return square(total)


def write_pieces(w_ref, line_ref, h_refs, pieces_ref, device, block):
    count = w_ref.shape[0]
    rows = w_ref.shape[1] // 2
    taps = count * LANES
    base = 0
    for (num, den), h_ref in zip(HARMONICS, h_refs):
        part_rows, part_cols = rows * num // den, block * num // den
        start = pl.multiple_of(device * part_cols, LANES)
        hankel(line_ref[:, pl.ds(start, part_cols + taps)], h_ref)
        pack = rows // part_rows
        if pack > 1:
            plane = packed(w_ref, h_ref, part_rows, part_cols, pack)
        else:
            left = weights(w_ref, range(count), part_rows)
            plane = jnp.concatenate(
                [
                    square(dot(left, hankel_tile(h_ref, col, range(count))))
                    for col in range(0, part_cols, TILE)
                ],
                1,
            )
        group = LANES * num
        wide = LANES * den
        groups = part_cols // group
        expand = (
            iota((group, wide), 1) * num // den == iota((group, wide), 0)
        ).astype(BF16)
        stacked = jnp.concatenate(
            [plane[:, g * group : (g + 1) * group] for g in range(groups)], 0
        )
        spread = dot(stacked, expand).astype(BF16)
        for g in range(groups):
            pieces_ref[base : base + part_rows, g * wide : (g + 1) * wide] = spread[
                g * part_rows : (g + 1) * part_rows
            ]
        base += part_rows


def fill_line(line_ref, blocks_ref, half, blocks):
    block = blocks_ref.shape[2]
    end = half + blocks * block
    line_ref[:, :half] = jnp.zeros((2, half), F32)
    for j in range(blocks):
        line_ref[:, half + j * block : half + (j + 1) * block] = blocks_ref[j].astype(F32)
    line_ref[:, end : end + half] = jnp.zeros((2, half), F32)


def pair_kernel(w_ref, own_ref, other_ref, pieces_ref, line_ref, *h_refs):
    block = own_ref.shape[1]
    half = w_ref.shape[0] * LANES // 2
    device = lax.axis_index("freq")

    @pl.when(device < 2)
    def _():
        line_ref[:, :half] = jnp.zeros((2, half), F32)
        mine = pl.multiple_of(half + device * block, LANES)
        theirs = pl.multiple_of(half + (1 - device) * block, LANES)
        line_ref[:, pl.ds(mine, block)] = own_ref[...].astype(F32)
        line_ref[:, pl.ds(theirs, block)] = other_ref[...].astype(F32)
        write_pieces(w_ref, line_ref, h_refs, pieces_ref, device, block)


def plane_kernel(
    w_ref, inner_ref, edge_ref, early_ref, all_ref, out_ref, line_ref, side_ref, pieces_ref, buffer_ref, sems, *h_refs
):
    owners, _, block = all_ref.shape
    rows = w_ref.shape[1] // 2
    count = w_ref.shape[0]
    half = count * LANES // 2
    device = lax.axis_index("freq")
    fill_line(line_ref, all_ref, half, owners)

    @pl.when(device < 2)
    def _():
        pieces_ref[...] = early_ref[...]

    @pl.when(device >= 2)
    def _():
        write_pieces(w_ref, line_ref, h_refs, pieces_ref, device, block)

    own = pl.multiple_of(device * block, LANES)
    edges = []
    pad = jnp.zeros((2, 2 * LANES), F32)
    hankel(jnp.concatenate([line_ref[:, pl.ds(own, half)], pad], 1), side_ref.at[0])
    after = pl.multiple_of(own + half + block, LANES)
    hankel(jnp.concatenate([pad, line_ref[:, pl.ds(after, half)], pad[:, :LANES]], 1), side_ref.at[1])
    for col in range(0, half, TILE):
        steps = [m for m in range(count) if col + m * LANES < half]
        edges.append(
            edge_ref[:, col : col + TILE]
            + dot(weights(w_ref, steps), hankel_tile(side_ref.at[0], col, steps))
        )
    shift = 2 * half - 2 * LANES
    for col in range(0, half, TILE):
        steps = [m for m in range(count) if col + m * LANES >= shift]
        edges.append(
            edge_ref[:, half + col : half + col + TILE]
            + dot(weights(w_ref, steps), hankel_tile(side_ref.at[1], col - shift, steps))
        )
    edges = [square(edge) for edge in edges]
    middle = len(edges) // 2
    own_plane = jnp.concatenate(edges[:middle] + [inner_ref[...]] + edges[middle:], 1)

    picks = jnp.concatenate(
        [
            (
                iota((rows, rows * num // den), 0) * num // den
                == iota((rows, rows * num // den), 1)
            ).astype(BF16)
            for num, den in HARMONICS
        ],
        1,
    )
    chunks = sems.shape[0]
    width = block // chunks
    copies = []
    for n in range(chunks):
        at = slice(n * width, (n + 1) * width)
        buffer_ref[:, at] = own_plane[:, at].astype(F32) + dot(picks, pieces_ref[:, at])
        copy = pltpu.make_async_copy(buffer_ref.at[:, at], out_ref.at[:, at], sems.at[n])
        copy.start()
        copies.append(copy)
    for copy in copies:
        copy.wait()


def body(spectrum, template_bank, template_index):
    owners = lax.axis_size("freq")
    block = spectrum.shape[1]
    rows = template_index.shape[0]
    taps = template_bank.shape[2]
    half = taps // 2
    all_pieces = sum(rows * num // den for num, den in HARMONICS)
    hankels = [
        pltpu.VMEM((2 * LANES, block * num // den + taps - LANES), BF16) for num, den in HARMONICS
    ]
    shared = pl.pallas_call(
        share_kernel,
        out_shape=pltpu.VMEM((owners, 2, block), BF16),
        in_specs=[VMEM],
        out_specs=VMEM,
        name="share",
    )(spectrum)
    everything = lax.all_to_all(shared, "freq", split_axis=0, concat_axis=0, tiled=True)
    other = lax.ppermute(spectrum, "freq", [(i, i ^ 1) for i in range(owners)])
    w, inner, edge = pl.pallas_call(
        local_kernel,
        out_shape=(
            jax.ShapeDtypeStruct((taps // LANES, 2 * rows, 2 * LANES), BF16),
            jax.ShapeDtypeStruct((rows, block - 2 * half), BF16),
            jax.ShapeDtypeStruct((2 * rows, 2 * half), F32),
        ),
        in_specs=[HBM] * 3,
        out_specs=(VMEM,) * 3,
        scratch_shapes=[
            pltpu.VMEM((1, rows), jnp.int32),
            pltpu.VMEM(template_bank.shape, BF16),
            pltpu.VMEM(spectrum.shape, BF16),
            pltpu.VMEM((2 * LANES, block + taps - LANES), BF16),
            pltpu.SemaphoreType.DMA((3,)),
        ],
        compiler_params=pltpu.CompilerParams(vmem_limit_bytes=24 << 20),
        name="local",
    )(template_index.reshape(1, rows), template_bank, spectrum)
    early = pl.pallas_call(
        pair_kernel,
        out_shape=jax.ShapeDtypeStruct((all_pieces, block), BF16),
        in_specs=[VMEM] * 3,
        out_specs=VMEM,
        scratch_shapes=[pltpu.VMEM((2, 2 * block + taps), F32)] + hankels,
        compiler_params=pltpu.CompilerParams(vmem_limit_bytes=24 << 20),
        name="pair",
    )(w, spectrum, other)
    return pl.pallas_call(
        plane_kernel,
        out_shape=jax.ShapeDtypeStruct((rows, block), F32),
        in_specs=[VMEM] * 5,
        out_specs=ANY,
        scratch_shapes=[
            pltpu.VMEM((2, owners * block + taps), F32),
            pltpu.VMEM((2, 2 * LANES, half + TILE), BF16),
            pltpu.VMEM((all_pieces, block), BF16),
            pltpu.VMEM((rows, block), F32),
            pltpu.SemaphoreType.DMA((4,)),
        ]
        + hankels,
        compiler_params=pltpu.CompilerParams(vmem_limit_bytes=32 << 20),
        name="plane",
    )(w, inner, edge, early, everything)


def solution(mesh):
    return jax.shard_map(
        body,
        mesh=mesh,
        in_specs=(P(None, ("beam", "freq")), P(), P()),
        out_specs=P(None, ("beam", "freq")),
        check_vma=False,
    )
```

```python
import jax
import jax.numpy as jnp
from jax import lax
from jax.experimental import pallas as pl
from jax.experimental.pallas import tpu as pltpu
from jax.sharding import PartitionSpec as P

LANES = 128
TILE = 256
HARMONICS = ((3, 4), (1, 2), (1, 4))
F32 = jnp.float32
BF16 = jnp.bfloat16
VMEM = pl.BlockSpec(memory_space=pltpu.VMEM)
ANY = pl.BlockSpec(memory_space=pl.ANY)


def iota(shape, dim):
    return lax.broadcasted_iota(jnp.int32, shape, dim)


def dot(left, right):
    return jnp.dot(left, right, preferred_element_type=F32)


def square(pair):
    rows = pair.shape[0] // 2
    re, im = pair[:rows], pair[rows:]
    return (re * re + im * im).astype(BF16)


def hankel(window, h_ref):
    length = window.shape[1]
    kept = length - LANES
    for c in range(2):
        row = jnp.broadcast_to(window[c : c + 1, :], (8, length))
        for a in range(0, LANES // 8, 2):
            pair = [
                pltpu.roll(row, length - 8 * k - 7, 1, stride=1, stride_axis=0)[:, :kept]
                for k in (a, a + 1)
            ]
            at = c * LANES + 8 * a
            h_ref[at : at + 16, :kept] = jnp.concatenate(pair, 0).astype(BF16)


def hankel_tile(h_ref, col, steps, width=TILE):
    return jnp.concatenate(
        [h_ref[:, col + m * LANES : col + m * LANES + width] for m in steps], 0
    )


def weights(w_ref, steps, rows=None):
    all_rows = w_ref.shape[1] // 2
    if rows is None:
        return jnp.concatenate([w_ref[m] for m in steps], 1)
    return jnp.concatenate(
        [
            jnp.concatenate([w_ref[m, :rows], w_ref[m, all_rows : all_rows + rows]], 0)
            for m in steps
        ],
        1,
    )


def first_kernel(mark_ref):
    mark_ref[...] = jnp.zeros(mark_ref.shape, F32)


def share_kernel(mark_ref, own_ref, index_ref, shared_ref, index_out_ref):
    for j in range(shared_ref.shape[0]):
        shared_ref[j] = own_ref[...]
    index_out_ref[...] = index_ref[...]


def local_kernel(index_ref, bank_ref, own_ref, w_ref, inner_ref, edge_ref, h_ref):
    rows = index_ref.shape[1]
    bank = bank_ref.shape[1]
    taps = bank_ref.shape[2]
    half = taps // 2
    block = own_ref.shape[1]
    count = taps // LANES
    order = iota((LANES, LANES), 1)
    order = (order // 8) * 8 + 7 - order % 8
    flip = (iota((LANES, LANES), 0) == order).astype(BF16)
    zeros = jnp.zeros((2, half), F32)
    hankel(jnp.concatenate([zeros, own_ref[...].astype(F32), zeros], 1), h_ref)
    picked = (iota((bank, rows), 0) == index_ref[...]).astype(BF16)
    for m in range(count):
        part = []
        for c in range(2):
            chunk = bank_ref[c, :, m * LANES : (m + 1) * LANES]
            chunk = dot(chunk, flip).astype(BF16)
            part.append(
                lax.dot_general(
                    picked, chunk, (((0,), (0,)), ((), ())), preferred_element_type=F32
                )
            )
        re, im = part
        w_ref[m, :rows, :LANES] = re.astype(BF16)
        w_ref[m, :rows, LANES:] = (-im).astype(BF16)
        w_ref[m, rows:, :LANES] = im.astype(BF16)
        w_ref[m, rows:, LANES:] = re.astype(BF16)
    for col in range(0, block, TILE):
        steps = [
            m
            for m in range(count)
            if col + m * LANES + TILE + LANES - 1 > half and col + m * LANES < half + block
        ]
        got = dot(weights(w_ref, steps), hankel_tile(h_ref, col, steps))
        if half <= col < block - half:
            inner_ref[:, col - half : col - half + TILE] = square(got)
        else:
            at = col if col < half else col - block + 2 * half
            edge_ref[:, at : at + TILE] = got


def packed(w_ref, h_ref, rows, cols, pack):
    count = w_ref.shape[0]
    all_rows = w_ref.shape[1] // 2
    long = cols + (pack - 1) * LANES
    tiles = []
    left = jnp.concatenate(
        [
            jnp.concatenate(
                [w_ref[m + k, base : base + rows] for k in range(pack) for base in (0, all_rows)],
                0,
            )
            for m in range(0, count, pack)
        ],
        1,
    )
    col = 0
    while col < long:
        width = min(TILE, long - col)
        tiles.append(dot(left, hankel_tile(h_ref, col, range(0, count, pack), width)))
        col += width
    got = jnp.concatenate(tiles, 1)
    total = got[: 2 * rows, :cols]
    for k in range(1, pack):
        total = total + got[2 * rows * k : 2 * rows * (k + 1), k * LANES : k * LANES + cols]
    return square(total)


def harmonic_plane(w_ref, line_ref, h_ref, device, num, den, block):
    count = w_ref.shape[0]
    rows = w_ref.shape[1] // 2
    part_rows, part_cols = rows * num // den, block * num // den
    start = pl.multiple_of(device * part_cols, LANES)
    hankel(line_ref[:, pl.ds(start, part_cols + count * LANES)], h_ref)
    pack = rows // part_rows
    if pack > 1:
        return packed(w_ref, h_ref, part_rows, part_cols, pack)
    left = weights(w_ref, range(count), part_rows)
    return jnp.concatenate(
        [
            square(dot(left, hankel_tile(h_ref, col, range(count))))
            for col in range(0, part_cols, TILE)
        ],
        1,
    )


def stretch(plane, num, den):
    part_rows, part_cols = plane.shape
    group = LANES * num
    wide = LANES * den
    groups = part_cols // group
    expand = (iota((group, wide), 1) * num // den == iota((group, wide), 0)).astype(BF16)
    stacked = jnp.concatenate([plane[:, g * group : (g + 1) * group] for g in range(groups)], 0)
    spread = dot(stacked, expand).astype(BF16)
    return jnp.concatenate([spread[g * part_rows : (g + 1) * part_rows] for g in range(groups)], 1)


def group_order(owners):
    first = owners * 3 // 4 - 1
    return (first, *(j for j in range(owners) if j != first))


def fill_line(line_ref, blocks_ref, half):
    owners, _, block = blocks_ref.shape
    end = half + owners * block
    line_ref[:, :half] = jnp.zeros((2, half), F32)
    for n, j in enumerate(group_order(owners)):
        line_ref[:, half + j * block : half + (j + 1) * block] = blocks_ref[n].astype(F32)
    line_ref[:, end : end + half] = jnp.zeros((2, half), F32)


def own_plane(w_ref, inner_ref, edge_ref, line_ref, side_ref, device, block):
    count = w_ref.shape[0]
    half = count * LANES // 2
    own = pl.multiple_of(device * block, LANES)
    edges = []
    pad = jnp.zeros((2, 2 * LANES), F32)
    hankel(jnp.concatenate([line_ref[:, pl.ds(own, half)], pad], 1), side_ref.at[0])
    after = pl.multiple_of(own + half + block, LANES)
    hankel(jnp.concatenate([pad, line_ref[:, pl.ds(after, half)], pad[:, :LANES]], 1), side_ref.at[1])
    for col in range(0, half, TILE):
        steps = [m for m in range(count) if col + m * LANES < half]
        edges.append(
            edge_ref[:, col : col + TILE]
            + dot(weights(w_ref, steps), hankel_tile(side_ref.at[0], col, steps))
        )
    shift = 2 * half - 2 * LANES
    for col in range(0, half, TILE):
        steps = [m for m in range(count) if col + m * LANES >= shift]
        edges.append(
            edge_ref[:, half + col : half + col + TILE]
            + dot(weights(w_ref, steps), hankel_tile(side_ref.at[1], col - shift, steps))
        )
    edges = [square(edge) for edge in edges]
    middle = len(edges) // 2
    return jnp.concatenate(edges[:middle] + [inner_ref[...]] + edges[middle:], 1)


def write_sum(own, pieces, out_ref, buffer_ref, sems):
    rows, block = buffer_ref.shape
    picks = jnp.concatenate(
        [
            (
                iota((rows, rows * num // den), 0) * num // den
                == iota((rows, rows * num // den), 1)
            ).astype(BF16)
            for num, den in HARMONICS
        ],
        1,
    )
    chunks = sems.shape[0]
    width = block // chunks
    copies = []
    for n in range(chunks):
        at = slice(n * width, (n + 1) * width)
        rest = dot(picks, jnp.concatenate([piece[:, at] for piece in pieces], 0))
        buffer_ref[:, at] = own[:, at].astype(F32) + rest
        copy = pltpu.make_async_copy(buffer_ref.at[:, at], out_ref.at[:, at], sems.at[n])
        copy.start()
        copies.append(copy)
    for copy in copies:
        copy.wait()


def plane_kernel(
    w_ref, inner_ref, edge_ref, all_ref, out_ref, line_ref, side_ref, buffer_ref, sems, *h_refs
):
    block = all_ref.shape[2]
    rows = w_ref.shape[1] // 2
    half = w_ref.shape[0] * LANES // 2
    device = lax.axis_index("freq")
    fill_line(line_ref, all_ref, half)

    @pl.when(device > 0)
    def _():
        pieces = [
            stretch(harmonic_plane(w_ref, line_ref, h_ref, device, num, den, block), num, den)
            for (num, den), h_ref in zip(HARMONICS, h_refs)
        ]
        own = own_plane(w_ref, inner_ref, edge_ref, line_ref, side_ref, device, block)
        write_sum(own, pieces, out_ref, buffer_ref, sems)

    @pl.when(device == 0)
    def _():
        own = own_plane(w_ref, inner_ref, edge_ref, line_ref, side_ref, 0, block)
        pieces = [
            stretch(own[: rows * num // den, : block * num // den], num, den)
            for num, den in HARMONICS
        ]
        write_sum(own, pieces, out_ref, buffer_ref, sems)


def body(spectrum, template_bank, template_index):
    owners = lax.axis_size("freq")
    block = spectrum.shape[1]
    rows = template_index.shape[0]
    taps = template_bank.shape[2]
    half = taps // 2
    hankels = [
        pltpu.VMEM((2 * LANES, block * num // den + taps - LANES), BF16) for num, den in HARMONICS
    ]
    mark = pl.pallas_call(
        first_kernel,
        out_shape=jax.ShapeDtypeStruct((8, LANES), F32),
        out_specs=VMEM,
        compiler_params=pltpu.CompilerParams(vmem_limit_bytes=1 << 20),
        cost_estimate=pl.CostEstimate(flops=4 * 10**9, bytes_accessed=16 << 20, transcendentals=0),
        name="first",
    )()
    shared, index = pl.pallas_call(
        share_kernel,
        out_shape=(
            jax.ShapeDtypeStruct((owners, 2, block), BF16),
            jax.ShapeDtypeStruct((1, rows), jnp.int32),
        ),
        in_specs=[ANY, VMEM, VMEM],
        out_specs=(VMEM,) * 2,
        compiler_params=pltpu.CompilerParams(vmem_limit_bytes=4 << 20),
        cost_estimate=pl.CostEstimate(flops=4 * 10**9, bytes_accessed=16 << 20, transcendentals=0),
        name="share",
    )(mark, spectrum, template_index.reshape(1, rows))
    everything = lax.all_to_all(
        shared,
        "freq",
        split_axis=0,
        concat_axis=0,
        tiled=True,
        axis_index_groups=[list(group_order(owners))],
    )
    w, inner, edge = pl.pallas_call(
        local_kernel,
        out_shape=(
            jax.ShapeDtypeStruct((taps // LANES, 2 * rows, 2 * LANES), BF16),
            jax.ShapeDtypeStruct((rows, block - 2 * half), BF16),
            jax.ShapeDtypeStruct((2 * rows, 2 * half), F32),
        ),
        in_specs=[VMEM] * 3,
        out_specs=(VMEM,) * 3,
        scratch_shapes=[pltpu.VMEM((2 * LANES, block + taps - LANES), BF16)],
        compiler_params=pltpu.CompilerParams(vmem_limit_bytes=24 << 20),
        name="local",
    )(index, template_bank, spectrum)
    return pl.pallas_call(
        plane_kernel,
        out_shape=jax.ShapeDtypeStruct((rows, block), F32),
        in_specs=[VMEM] * 4,
        out_specs=ANY,
        scratch_shapes=[
            pltpu.VMEM((2, owners * block + taps), F32),
            pltpu.VMEM((2, 2 * LANES, half + TILE), BF16),
            pltpu.VMEM((rows, block), F32),
            pltpu.SemaphoreType.DMA((4,)),
        ]
        + hankels,
        compiler_params=pltpu.CompilerParams(vmem_limit_bytes=32 << 20),
        name="plane",
    )(w, inner, edge, everything)


def solution(mesh):
    return jax.shard_map(
        body,
        mesh=mesh,
        in_specs=(P(None, ("beam", "freq")), P(), P()),
        out_specs=P(None, ("beam", "freq")),
        check_vma=False,
    )
```

```python
import math

import jax
import jax.numpy as jnp
from jax import lax
from jax.experimental import pallas as pl
from jax.experimental.pallas import tpu as pltpu
from jax.sharding import PartitionSpec as P

LANES = 128
TILE = 256
HARMONICS = ((3, 4), (1, 2), (1, 4))
F32 = jnp.float32
BF16 = jnp.bfloat16
VMEM = pl.BlockSpec(memory_space=pltpu.VMEM)
ANY = pl.BlockSpec(memory_space=pl.ANY)


def iota(shape, dim):
    return lax.broadcasted_iota(jnp.int32, shape, dim)


def dot(left, right):
    return jnp.dot(left, right, preferred_element_type=F32)


def square(pair):
    rows = pair.shape[0] // 2
    re, im = pair[:rows], pair[rows:]
    return (re * re + im * im).astype(BF16)


def hankel(window, h_ref):
    length = window.shape[1]
    kept = length - LANES
    for c in range(2):
        row = jnp.broadcast_to(window[c : c + 1, :], (8, length))
        for a in range(0, LANES // 8, 2):
            pair = [
                pltpu.roll(row, length - 8 * k - 7, 1, stride=1, stride_axis=0)[:, :kept]
                for k in (a, a + 1)
            ]
            at = c * LANES + 8 * a
            h_ref[at : at + 16, :kept] = jnp.concatenate(pair, 0).astype(BF16)


def hankel_tile(h_ref, col, steps, width=TILE):
    return jnp.concatenate(
        [h_ref[:, col + m * LANES : col + m * LANES + width] for m in steps], 0
    )


def weights(w_ref, steps, rows=None):
    all_rows = w_ref.shape[1] // 2
    if rows is None:
        return jnp.concatenate([w_ref[m] for m in steps], 1)
    return jnp.concatenate(
        [
            jnp.concatenate([w_ref[m, :rows], w_ref[m, all_rows : all_rows + rows]], 0)
            for m in steps
        ],
        1,
    )


def first_kernel(mark_ref):
    mark_ref[...] = jnp.zeros(mark_ref.shape, F32)


def share_kernel(mark_ref, own_ref, index_ref, shared_ref, index_out_ref):
    for j in range(shared_ref.shape[0]):
        shared_ref[j] = own_ref[...]
    index_out_ref[...] = index_ref[...]


def local_kernel(index_ref, bank_ref, own_ref, w_ref, inner_ref, edge_ref, h_ref):
    rows = index_ref.shape[1]
    bank = bank_ref.shape[1]
    taps = bank_ref.shape[2]
    half = taps // 2
    block = own_ref.shape[1]
    count = taps // LANES
    order = iota((LANES, LANES), 1)
    order = (order // 8) * 8 + 7 - order % 8
    flip = (iota((LANES, LANES), 0) == order).astype(BF16)
    zeros = jnp.zeros((2, half), F32)
    hankel(jnp.concatenate([zeros, own_ref[...].astype(F32), zeros], 1), h_ref)
    picked = (iota((bank, rows), 0) == index_ref[...]).astype(BF16)
    for m in range(count):
        part = []
        for c in range(2):
            chunk = bank_ref[c, :, m * LANES : (m + 1) * LANES]
            chunk = dot(chunk, flip).astype(BF16)
            part.append(
                lax.dot_general(
                    picked, chunk, (((0,), (0,)), ((), ())), preferred_element_type=F32
                )
            )
        re, im = part
        w_ref[m, :rows, :LANES] = re.astype(BF16)
        w_ref[m, :rows, LANES:] = (-im).astype(BF16)
        w_ref[m, rows:, :LANES] = im.astype(BF16)
        w_ref[m, rows:, LANES:] = re.astype(BF16)
    for col in range(0, block, TILE):
        steps = [
            m
            for m in range(count)
            if col + m * LANES + TILE + LANES - 1 > half and col + m * LANES < half + block
        ]
        got = dot(weights(w_ref, steps), hankel_tile(h_ref, col, steps))
        if half <= col < block - half:
            inner_ref[:, col - half : col - half + TILE] = square(got)
        else:
            at = col if col < half else col - block + 2 * half
            edge_ref[:, at : at + TILE] = got


def packed(w_ref, h_ref, rows, cols, pack):
    count = w_ref.shape[0]
    all_rows = w_ref.shape[1] // 2
    long = cols + (pack - 1) * LANES
    tiles = []
    left = jnp.concatenate(
        [
            jnp.concatenate(
                [w_ref[m + k, base : base + rows] for k in range(pack) for base in (0, all_rows)],
                0,
            )
            for m in range(0, count, pack)
        ],
        1,
    )
    col = 0
    while col < long:
        width = min(TILE, long - col)
        tiles.append(dot(left, hankel_tile(h_ref, col, range(0, count, pack), width)))
        col += width
    got = jnp.concatenate(tiles, 1)
    total = got[: 2 * rows, :cols]
    for k in range(1, pack):
        total = total + got[2 * rows * k : 2 * rows * (k + 1), k * LANES : k * LANES + cols]
    return square(total)


def harmonic_plane(w_ref, all_ref, h_ref, device, unit, num, den):
    count = w_ref.shape[0]
    rows = w_ref.shape[1] // 2
    taps = count * LANES
    part_rows, part_cols = rows * num // den, all_ref.shape[2] * num // den
    start = device * (part_cols // unit) - taps // 2 // unit
    hankel(bins(all_ref, unit, start, (part_cols + taps) // unit), h_ref)
    pack = rows // part_rows
    if pack > 1:
        return packed(w_ref, h_ref, part_rows, part_cols, min(pack, 2))
    left = weights(w_ref, range(count), part_rows)
    return jnp.concatenate(
        [
            square(dot(left, hankel_tile(h_ref, col, range(count))))
            for col in range(0, part_cols, TILE)
        ],
        1,
    )


def stretch(plane, num, den):
    part_rows, part_cols = plane.shape
    tiles = part_cols * den // num // TILE
    starts = [j * TILE * num // den for j in range(tiles)]
    wide = -(-(max(start % LANES for start in starts) + TILE * num // den) // LANES) * LANES
    done = {}
    for offset in sorted({start % LANES for start in starts}):
        members = [j for j in range(tiles) if starts[j] % LANES == offset]
        expand = (
            iota((wide, TILE), 1) * num // den + offset == iota((wide, TILE), 0)
        ).astype(BF16)
        bases = [starts[j] - offset for j in members]
        stacked = jnp.concatenate([plane[:, base : base + wide] for base in bases], 0)
        spread = dot(stacked, expand).astype(BF16)
        for n, j in enumerate(members):
            done[j] = spread[n * part_rows : (n + 1) * part_rows]
    return jnp.concatenate([done[j] for j in range(tiles)], 1)


def group_order(owners):
    first = owners * 3 // 4 - 1
    return (first, *(j for j in range(owners) if j != first))


def bins(all_ref, unit, start, count):
    owners, _, block = all_ref.shape
    per = block // unit
    first = group_order(owners)[0]
    got = []
    for k in range(count):
        at = start + k
        inside = jnp.logical_and(at >= 0, at < owners * per)
        at = jnp.clip(at, 0, owners * per - 1)
        owner = at // per
        slot = jnp.where(owner == first, 0, jnp.where(owner < first, owner + 1, owner))
        column = pl.multiple_of((at - owner * per) * unit, LANES)
        piece = all_ref[slot, :, pl.ds(column, unit)].astype(F32)
        got.append(jnp.where(inside, piece, 0.0))
    return jnp.concatenate(got, 1)


def own_plane(w_ref, inner_ref, edge_ref, all_ref, side_ref, device, unit):
    count = w_ref.shape[0]
    half = count * LANES // 2
    width = half // unit
    here = device * (all_ref.shape[2] // unit)
    edges = []
    pad = jnp.zeros((2, 2 * LANES), F32)
    before = bins(all_ref, unit, here - width, width)
    hankel(jnp.concatenate([before, pad], 1), side_ref.at[0])
    after = bins(all_ref, unit, here + all_ref.shape[2] // unit, width)
    hankel(jnp.concatenate([pad, after, pad[:, :LANES]], 1), side_ref.at[1])
    for col in range(0, half, TILE):
        steps = [m for m in range(count) if col + m * LANES < half]
        edges.append(
            edge_ref[:, col : col + TILE]
            + dot(weights(w_ref, steps), hankel_tile(side_ref.at[0], col, steps))
        )
    shift = 2 * half - 2 * LANES
    for col in range(0, half, TILE):
        steps = [m for m in range(count) if col + m * LANES >= shift]
        edges.append(
            edge_ref[:, half + col : half + col + TILE]
            + dot(weights(w_ref, steps), hankel_tile(side_ref.at[1], col - shift, steps))
        )
    edges = [square(edge) for edge in edges]
    middle = len(edges) // 2
    return jnp.concatenate(edges[:middle] + [inner_ref[...]] + edges[middle:], 1)


def write_sum(own, pieces, out_ref, buffer_ref, sems):
    rows, block = buffer_ref.shape
    picks = jnp.concatenate(
        [
            (
                iota((rows, rows * num // den), 0) * num // den
                == iota((rows, rows * num // den), 1)
            ).astype(BF16)
            for num, den in HARMONICS
        ],
        1,
    )
    chunks = sems.shape[0]
    width = block // chunks
    copies = []
    for n in range(chunks):
        at = slice(n * width, (n + 1) * width)
        rest = dot(picks, jnp.concatenate([piece[:, at] for piece in pieces], 0))
        buffer_ref[:, at] = own[:, at].astype(F32) + rest
        copy = pltpu.make_async_copy(buffer_ref.at[:, at], out_ref.at[:, at], sems.at[n])
        copy.start()
        copies.append(copy)
    for copy in copies:
        copy.wait()


def plane_kernel(
    w_ref, inner_ref, edge_ref, all_ref, out_ref, side_ref, buffer_ref, sems, *h_refs
):
    block = all_ref.shape[2]
    rows = w_ref.shape[1] // 2
    half = w_ref.shape[0] * LANES // 2
    device = lax.axis_index("freq")
    unit = math.gcd(half, *(block * num // den for num, den in HARMONICS))

    @pl.when(device > 0)
    def _():
        planes = [
            harmonic_plane(w_ref, all_ref, h_ref, device, unit, num, den)
            for (num, den), h_ref in zip(HARMONICS, h_refs)
        ]
        pieces = [stretch(plane, num, den) for plane, (num, den) in zip(planes, HARMONICS)]
        own = own_plane(w_ref, inner_ref, edge_ref, all_ref, side_ref, device, unit)
        write_sum(own, pieces, out_ref, buffer_ref, sems)

    @pl.when(device == 0)
    def _():
        own = own_plane(w_ref, inner_ref, edge_ref, all_ref, side_ref, device, unit)
        pieces = [
            stretch(own[: rows * num // den, : block * num // den], num, den)
            for num, den in HARMONICS
        ]
        write_sum(own, pieces, out_ref, buffer_ref, sems)


def body(spectrum, template_bank, template_index):
    owners = lax.axis_size("freq")
    block = spectrum.shape[1]
    rows = template_index.shape[0]
    taps = template_bank.shape[2]
    half = taps // 2
    hankels = [
        pltpu.VMEM((2 * LANES, block * num // den + taps - LANES), BF16) for num, den in HARMONICS
    ]
    mark = pl.pallas_call(
        first_kernel,
        out_shape=jax.ShapeDtypeStruct((8, LANES), F32),
        out_specs=VMEM,
        compiler_params=pltpu.CompilerParams(vmem_limit_bytes=1 << 20),
        cost_estimate=pl.CostEstimate(flops=4 * 10**9, bytes_accessed=16 << 20, transcendentals=0),
        name="first",
    )()
    shared, index = pl.pallas_call(
        share_kernel,
        out_shape=(
            jax.ShapeDtypeStruct((owners, 2, block), BF16),
            jax.ShapeDtypeStruct((1, rows), jnp.int32),
        ),
        in_specs=[ANY, VMEM, VMEM],
        out_specs=(VMEM,) * 2,
        compiler_params=pltpu.CompilerParams(vmem_limit_bytes=4 << 20),
        cost_estimate=pl.CostEstimate(flops=4 * 10**9, bytes_accessed=16 << 20, transcendentals=0),
        name="share",
    )(mark, spectrum, template_index.reshape(1, rows))
    everything = lax.all_to_all(
        shared,
        "freq",
        split_axis=0,
        concat_axis=0,
        tiled=True,
        axis_index_groups=[list(group_order(owners))],
    )
    w, inner, edge = pl.pallas_call(
        local_kernel,
        out_shape=(
            jax.ShapeDtypeStruct((taps // LANES, 2 * rows, 2 * LANES), BF16),
            jax.ShapeDtypeStruct((rows, block - 2 * half), BF16),
            jax.ShapeDtypeStruct((2 * rows, 2 * half), F32),
        ),
        in_specs=[VMEM] * 3,
        out_specs=(VMEM,) * 3,
        scratch_shapes=[pltpu.VMEM((2 * LANES, block + taps - LANES), BF16)],
        compiler_params=pltpu.CompilerParams(vmem_limit_bytes=24 << 20),
        name="local",
    )(index, template_bank, spectrum)
    return pl.pallas_call(
        plane_kernel,
        out_shape=jax.ShapeDtypeStruct((rows, block), F32),
        in_specs=[VMEM] * 4,
        out_specs=ANY,
        scratch_shapes=[
            pltpu.VMEM((2, 2 * LANES, half + TILE), BF16),
            pltpu.VMEM((rows, block), F32),
            pltpu.SemaphoreType.DMA((4,)),
        ]
        + hankels,
        compiler_params=pltpu.CompilerParams(vmem_limit_bytes=32 << 20),
        name="plane",
    )(w, inner, edge, everything)


def solution(mesh):
    return jax.shard_map(
        body,
        mesh=mesh,
        in_specs=(P(None, ("beam", "freq")), P(), P()),
        out_specs=P(None, ("beam", "freq")),
        check_vma=False,
    )
```

```python
import math

import jax
import jax.numpy as jnp
from jax import lax
from jax.experimental import pallas as pl
from jax.experimental.pallas import tpu as pltpu
from jax.sharding import PartitionSpec as P

LANES = 128
TILE = 256
HARMONICS = ((3, 4), (1, 2), (1, 4))
F32 = jnp.float32
BF16 = jnp.bfloat16
VMEM = pl.BlockSpec(memory_space=pltpu.VMEM)
ANY = pl.BlockSpec(memory_space=pl.ANY)


def iota(shape, dim):
    return lax.broadcasted_iota(jnp.int32, shape, dim)


def dot(left, right):
    return jnp.dot(left, right, preferred_element_type=F32)


def square(pair):
    rows = pair.shape[0] // 2
    re, im = pair[:rows], pair[rows:]
    return (re * re + im * im).astype(BF16)


def hankel(window, h_ref):
    length = window.shape[1]
    kept = length - LANES
    for c in range(2):
        row = jnp.broadcast_to(window[c : c + 1, :], (8, length))
        for a in range(0, LANES // 8, 2):
            pair = [
                pltpu.roll(row, length - 8 * k - 7, 1, stride=1, stride_axis=0)[:, :kept]
                for k in (a, a + 1)
            ]
            at = c * LANES + 8 * a
            h_ref[at : at + 16, :kept] = jnp.concatenate(pair, 0).astype(BF16)


def hankel_tile(h_ref, col, steps, width=TILE):
    return jnp.concatenate(
        [h_ref[:, col + m * LANES : col + m * LANES + width] for m in steps], 0
    )


def weights(w_ref, steps, rows=None):
    all_rows = w_ref.shape[1] // 2
    if rows is None:
        return jnp.concatenate([w_ref[m] for m in steps], 1)
    return jnp.concatenate(
        [
            jnp.concatenate([w_ref[m, :rows], w_ref[m, all_rows : all_rows + rows]], 0)
            for m in steps
        ],
        1,
    )


def first_kernel(mark_ref):
    mark_ref[...] = jnp.zeros(mark_ref.shape, F32)


def share_kernel(mark_ref, own_ref, index_ref, shared_ref, index_out_ref):
    for j in range(shared_ref.shape[0]):
        shared_ref[j] = own_ref[...]
    index_out_ref[...] = index_ref[...]


def local_kernel(index_ref, bank_ref, own_ref, w_ref, inner_ref, edge_ref, h_ref):
    rows = index_ref.shape[1]
    bank = bank_ref.shape[1]
    taps = bank_ref.shape[2]
    half = taps // 2
    block = own_ref.shape[1]
    count = taps // LANES
    order = iota((LANES, LANES), 1)
    order = (order // 8) * 8 + 7 - order % 8
    flip = (iota((LANES, LANES), 0) == order).astype(BF16)
    zeros = jnp.zeros((2, half), F32)
    hankel(jnp.concatenate([zeros, own_ref[...].astype(F32), zeros], 1), h_ref)
    picked = (iota((bank, rows), 0) == index_ref[...]).astype(BF16)
    for m in range(count):
        part = []
        for c in range(2):
            chunk = bank_ref[c, :, m * LANES : (m + 1) * LANES]
            chunk = dot(chunk, flip).astype(BF16)
            part.append(
                lax.dot_general(
                    picked, chunk, (((0,), (0,)), ((), ())), preferred_element_type=F32
                )
            )
        re, im = part
        w_ref[m, :rows, :LANES] = re.astype(BF16)
        w_ref[m, :rows, LANES:] = (-im).astype(BF16)
        w_ref[m, rows:, :LANES] = im.astype(BF16)
        w_ref[m, rows:, LANES:] = re.astype(BF16)
    for col in range(0, block, TILE):
        steps = [
            m
            for m in range(count)
            if col + m * LANES + TILE + LANES - 1 > half and col + m * LANES < half + block
        ]
        got = dot(weights(w_ref, steps), hankel_tile(h_ref, col, steps))
        if half <= col < block - half:
            inner_ref[:, col - half : col - half + TILE] = square(got)
        else:
            at = col if col < half else col - block + 2 * half
            edge_ref[:, at : at + TILE] = got


def packed(w_ref, h_ref, rows, cols, pack):
    count = w_ref.shape[0]
    all_rows = w_ref.shape[1] // 2
    steps = range(0, count, pack)
    left = jnp.concatenate(
        [
            jnp.concatenate(
                [w_ref[m + k, base : base + rows] for k in range(pack) for base in (0, all_rows)],
                0,
            )
            for m in steps
        ],
        1,
    )
    if pack == 1:
        return jnp.concatenate(
            [square(dot(left, hankel_tile(h_ref, col, steps))) for col in range(0, cols, TILE)], 1
        )
    done = []
    for col in range(0, cols, TILE):
        got = dot(left, hankel_tile(h_ref, col, steps))
        high = got[2 * rows :]
        if col > 0:
            done.append(square(low + jnp.concatenate([rest, high[:, :LANES]], 1)))
        low, rest = got[: 2 * rows], high[:, LANES:]
    high = dot(left[2 * rows :], hankel_tile(h_ref, cols, steps, LANES))
    done.append(square(low + jnp.concatenate([rest, high], 1)))
    return jnp.concatenate(done, 1)


def harmonic_plane(w_ref, all_ref, h_ref, device, unit, num, den):
    count = w_ref.shape[0]
    rows = w_ref.shape[1] // 2
    taps = count * LANES
    part_rows, part_cols = rows * num // den, all_ref.shape[2] * num // den
    start = device * (part_cols // unit) - taps // 2 // unit
    hankel(bins(all_ref, unit, start, (part_cols + taps) // unit), h_ref)
    return packed(w_ref, h_ref, part_rows, part_cols, min(2, rows // part_rows))


def stretch(plane, num, den):
    part_rows, part_cols = plane.shape
    tiles = part_cols * den // num // TILE
    starts = [j * TILE * num // den for j in range(tiles)]
    wide = -(-(max(start % LANES for start in starts) + TILE * num // den) // LANES) * LANES
    done = {}
    for offset in sorted({start % LANES for start in starts}):
        members = [j for j in range(tiles) if starts[j] % LANES == offset]
        expand = (
            iota((wide, TILE), 1) * num // den + offset == iota((wide, TILE), 0)
        ).astype(BF16)
        bases = [starts[j] - offset for j in members]
        stacked = jnp.concatenate([plane[:, base : base + wide] for base in bases], 0)
        spread = dot(stacked, expand).astype(BF16)
        for n, j in enumerate(members):
            done[j] = spread[n * part_rows : (n + 1) * part_rows]
    return jnp.concatenate([done[j] for j in range(tiles)], 1)


def group_order(owners):
    first = owners * 3 // 4 - 1
    return (first, *(j for j in range(owners) if j != first))


def bins(all_ref, unit, start, count):
    owners, _, block = all_ref.shape
    per = block // unit
    first = group_order(owners)[0]
    got = []
    for k in range(count):
        at = start + k
        inside = jnp.logical_and(at >= 0, at < owners * per)
        at = jnp.clip(at, 0, owners * per - 1)
        owner = at // per
        slot = jnp.where(owner == first, 0, jnp.where(owner < first, owner + 1, owner))
        column = pl.multiple_of((at - owner * per) * unit, LANES)
        piece = all_ref[slot, :, pl.ds(column, unit)].astype(F32)
        got.append(jnp.where(inside, piece, 0.0))
    return jnp.concatenate(got, 1)


def own_plane(w_ref, inner_ref, edge_ref, all_ref, side_ref, device, unit):
    count = w_ref.shape[0]
    half = count * LANES // 2
    width = half // unit
    here = device * (all_ref.shape[2] // unit)
    edges = []
    pad = jnp.zeros((2, 2 * LANES), F32)
    before = bins(all_ref, unit, here - width, width)
    hankel(jnp.concatenate([before, pad], 1), side_ref.at[0])
    after = bins(all_ref, unit, here + all_ref.shape[2] // unit, width)
    hankel(jnp.concatenate([pad, after, pad[:, :LANES]], 1), side_ref.at[1])
    for col in range(0, half, TILE):
        steps = [m for m in range(count) if col + m * LANES < half]
        edges.append(
            edge_ref[:, col : col + TILE]
            + dot(weights(w_ref, steps), hankel_tile(side_ref.at[0], col, steps))
        )
    shift = 2 * half - 2 * LANES
    for col in range(0, half, TILE):
        steps = [m for m in range(count) if col + m * LANES >= shift]
        edges.append(
            edge_ref[:, half + col : half + col + TILE]
            + dot(weights(w_ref, steps), hankel_tile(side_ref.at[1], col - shift, steps))
        )
    edges = [square(edge) for edge in edges]
    middle = len(edges) // 2
    return jnp.concatenate(edges[:middle] + [inner_ref[...]] + edges[middle:], 1)


def write_sum(own, pieces, out_ref, buffer_ref, sems):
    rows, block = buffer_ref.shape
    picks = jnp.concatenate(
        [
            (
                iota((rows, rows * num // den), 0) * num // den
                == iota((rows, rows * num // den), 1)
            ).astype(BF16)
            for num, den in HARMONICS
        ],
        1,
    )
    chunks = sems.shape[0]
    width = block // chunks
    copies = []
    for n in range(chunks):
        at = slice(n * width, (n + 1) * width)
        rest = dot(picks, jnp.concatenate([piece[:, at] for piece in pieces], 0))
        buffer_ref[:, at] = own[:, at].astype(F32) + rest
        copy = pltpu.make_async_copy(buffer_ref.at[:, at], out_ref.at[:, at], sems.at[n])
        copy.start()
        copies.append(copy)
    for copy in copies:
        copy.wait()


def plane_kernel(
    w_ref, inner_ref, edge_ref, all_ref, out_ref, side_ref, buffer_ref, sems, *h_refs
):
    block = all_ref.shape[2]
    rows = w_ref.shape[1] // 2
    half = w_ref.shape[0] * LANES // 2
    device = lax.axis_index("freq")
    unit = math.gcd(half, *(block * num // den for num, den in HARMONICS))

    @pl.when(device > 0)
    def _():
        planes = [
            harmonic_plane(w_ref, all_ref, h_ref, device, unit, num, den)
            for (num, den), h_ref in zip(HARMONICS, h_refs)
        ]
        pieces = [stretch(plane, num, den) for plane, (num, den) in zip(planes, HARMONICS)]
        own = own_plane(w_ref, inner_ref, edge_ref, all_ref, side_ref, device, unit)
        write_sum(own, pieces, out_ref, buffer_ref, sems)

    @pl.when(device == 0)
    def _():
        own = own_plane(w_ref, inner_ref, edge_ref, all_ref, side_ref, device, unit)
        pieces = [
            stretch(own[: rows * num // den, : block * num // den], num, den)
            for num, den in HARMONICS
        ]
        write_sum(own, pieces, out_ref, buffer_ref, sems)


def body(spectrum, template_bank, template_index):
    owners = lax.axis_size("freq")
    block = spectrum.shape[1]
    rows = template_index.shape[0]
    taps = template_bank.shape[2]
    half = taps // 2
    hankels = [
        pltpu.VMEM((2 * LANES, block * num // den + taps - LANES), BF16) for num, den in HARMONICS
    ]
    mark = pl.pallas_call(
        first_kernel,
        out_shape=jax.ShapeDtypeStruct((8, LANES), F32),
        out_specs=VMEM,
        compiler_params=pltpu.CompilerParams(vmem_limit_bytes=1 << 20),
        cost_estimate=pl.CostEstimate(flops=4 * 10**9, bytes_accessed=16 << 20, transcendentals=0),
        name="first",
    )()
    shared, index = pl.pallas_call(
        share_kernel,
        out_shape=(
            jax.ShapeDtypeStruct((owners, 2, block), BF16),
            jax.ShapeDtypeStruct((1, rows), jnp.int32),
        ),
        in_specs=[ANY, VMEM, VMEM],
        out_specs=(VMEM,) * 2,
        compiler_params=pltpu.CompilerParams(vmem_limit_bytes=4 << 20),
        cost_estimate=pl.CostEstimate(flops=4 * 10**9, bytes_accessed=16 << 20, transcendentals=0),
        name="share",
    )(mark, spectrum, template_index.reshape(1, rows))
    everything = lax.all_to_all(
        shared,
        "freq",
        split_axis=0,
        concat_axis=0,
        tiled=True,
        axis_index_groups=[list(group_order(owners))],
    )
    w, inner, edge = pl.pallas_call(
        local_kernel,
        out_shape=(
            jax.ShapeDtypeStruct((taps // LANES, 2 * rows, 2 * LANES), BF16),
            jax.ShapeDtypeStruct((rows, block - 2 * half), BF16),
            jax.ShapeDtypeStruct((2 * rows, 2 * half), F32),
        ),
        in_specs=[VMEM] * 3,
        out_specs=(VMEM,) * 3,
        scratch_shapes=[pltpu.VMEM((2 * LANES, block + taps - LANES), BF16)],
        compiler_params=pltpu.CompilerParams(vmem_limit_bytes=24 << 20),
        name="local",
    )(index, template_bank, spectrum)
    return pl.pallas_call(
        plane_kernel,
        out_shape=jax.ShapeDtypeStruct((rows, block), F32),
        in_specs=[VMEM] * 4,
        out_specs=ANY,
        scratch_shapes=[
            pltpu.VMEM((2, 2 * LANES, half + TILE), BF16),
            pltpu.VMEM((rows, block), F32),
            pltpu.SemaphoreType.DMA((4,)),
        ]
        + hankels,
        compiler_params=pltpu.CompilerParams(vmem_limit_bytes=32 << 20),
        name="plane",
    )(w, inner, edge, everything)


def solution(mesh):
    return jax.shard_map(
        body,
        mesh=mesh,
        in_specs=(P(None, ("beam", "freq")), P(), P()),
        out_specs=P(None, ("beam", "freq")),
        check_vma=False,
    )
```

```python
import math

import jax
import jax.numpy as jnp
from jax import lax
from jax.experimental import pallas as pl
from jax.experimental.pallas import tpu as pltpu
from jax.sharding import PartitionSpec as P

LANES = 128
TILE = 256
HARMONICS = ((3, 4), (1, 2), (1, 4))
HELD = HARMONICS[:1]
F32 = jnp.float32
BF16 = jnp.bfloat16
VMEM = pl.BlockSpec(memory_space=pltpu.VMEM)
ANY = pl.BlockSpec(memory_space=pl.ANY)


def iota(shape, dim):
    return lax.broadcasted_iota(jnp.int32, shape, dim)


def dot(left, right):
    return jnp.dot(left, right, preferred_element_type=F32)


def square(pair):
    rows = pair.shape[0] // 2
    re, im = pair[:rows], pair[rows:]
    return (re * re + im * im).astype(BF16)


def hankel(window, h_ref):
    length = window.shape[1]
    kept = length - LANES
    for c in range(2):
        row = jnp.broadcast_to(window[c : c + 1, :], (8, length))
        for a in range(0, LANES // 8, 2):
            pair = [
                pltpu.roll(row, length - 8 * k - 7, 1, stride=1, stride_axis=0)[:, :kept]
                for k in (a, a + 1)
            ]
            at = c * LANES + 8 * a
            h_ref[at : at + 16, :kept] = jnp.concatenate(pair, 0).astype(BF16)


def hankel_tile(h_ref, col, steps, width=TILE):
    return jnp.concatenate(
        [h_ref[:, col + m * LANES : col + m * LANES + width] for m in steps], 0
    )


def half_step(w_ref, m, part, rows):
    all_rows = w_ref.shape[1] // 3
    picked = ((0, 2), (1, 0))[part]
    return jnp.concatenate([w_ref[m, k * all_rows : k * all_rows + rows, :] for k in picked], 1)


def weights(w_ref, steps):
    rows = w_ref.shape[1] // 3
    return jnp.concatenate(
        [
            jnp.concatenate([half_step(w_ref, m, part, rows) for part in (0, 1)], 0)
            for m in steps
        ],
        1,
    )


def first_kernel(mark_ref):
    mark_ref[...] = jnp.zeros(mark_ref.shape, F32)


def share_kernel(mark_ref, own_ref, index_ref, shared_ref, index_out_ref):
    for j in range(shared_ref.shape[0]):
        shared_ref[j] = own_ref[...]
    index_out_ref[...] = index_ref[...]


def local_kernel(
    index_ref, bank_ref, own_ref, w_ref, inner_ref, edge_ref, picks_ref, expand_ref, h_ref
):
    rows = index_ref.shape[1]
    bank = bank_ref.shape[1]
    taps = bank_ref.shape[2]
    half = taps // 2
    block = own_ref.shape[1]
    count = taps // LANES
    order = iota((LANES, LANES), 1)
    order = (order // 8) * 8 + 7 - order % 8
    flip = (iota((LANES, LANES), 0) == order).astype(BF16)
    zeros = jnp.zeros((2, half), F32)
    hankel(jnp.concatenate([zeros, own_ref[...].astype(F32), zeros], 1), h_ref)
    picked = (iota((bank, rows), 0) == index_ref[...]).astype(BF16)
    for m in range(count):
        part = []
        for c in range(2):
            chunk = bank_ref[c, :, m * LANES : (m + 1) * LANES]
            chunk = dot(chunk, flip).astype(BF16)
            part.append(
                lax.dot_general(
                    picked, chunk, (((0,), (0,)), ((), ())), preferred_element_type=F32
                )
            )
        re, im = part
        w_ref[m, :rows] = re.astype(BF16)
        w_ref[m, rows : 2 * rows] = im.astype(BF16)
        w_ref[m, 2 * rows :] = (-im).astype(BF16)
    write_constants(picks_ref, expand_ref, block)
    for col in range(0, block, TILE):
        steps = [
            m
            for m in range(count)
            if col + m * LANES + TILE + LANES - 1 > half and col + m * LANES < half + block
        ]
        got = dot(weights(w_ref, steps), hankel_tile(h_ref, col, steps))
        if half <= col < block - half:
            inner_ref[:, col - half : col - half + TILE] = square(got)
        else:
            at = col if col < half else col - block + 2 * half
            edge_ref[:, at : at + TILE] = got


def packed(w_ref, h_ref, rows, cols, pack):
    count = w_ref.shape[0]
    all_rows = w_ref.shape[1] // 3
    steps = range(0, count, pack)
    left = jnp.concatenate(
        [
            jnp.concatenate(
                [half_step(w_ref, m + k, part, rows) for k in range(pack) for part in (0, 1)],
                0,
            )
            for m in steps
        ],
        1,
    )
    if pack == 1:
        return jnp.concatenate(
            [square(dot(left, hankel_tile(h_ref, col, steps))) for col in range(0, cols, TILE)], 1
        )
    done = []
    for col in range(0, cols, TILE):
        got = dot(left, hankel_tile(h_ref, col, steps))
        high = got[2 * rows :]
        if col > 0:
            done.append(square(low + jnp.concatenate([rest, high[:, :LANES]], 1)))
        low, rest = got[: 2 * rows], high[:, LANES:]
    high = dot(left[2 * rows :], hankel_tile(h_ref, cols, steps, LANES))
    done.append(square(low + jnp.concatenate([rest, high], 1)))
    return jnp.concatenate(done, 1)


def harmonic_plane(w_ref, all_ref, h_ref, device, unit, num, den):
    count = w_ref.shape[0]
    rows = w_ref.shape[1] // 3
    taps = count * LANES
    part_rows, part_cols = rows * num // den, all_ref.shape[2] * num // den
    start = device * (part_cols // unit) - taps // 2 // unit
    hankel(bins(all_ref, unit, start, (part_cols + taps) // unit), h_ref)
    return packed(w_ref, h_ref, part_rows, part_cols, min(2, rows // part_rows))


def stretch_plan(part_cols, num, den):
    tiles = part_cols * den // num // TILE
    starts = [j * TILE * num // den for j in range(tiles)]
    offsets = sorted({start % LANES for start in starts})
    wide = -(-(max(offsets) + TILE * num // den) // LANES) * LANES
    return starts, offsets, wide


def expands(block):
    got = {}
    base = 0
    for num, den in HELD:
        _, offsets, wide = stretch_plan(block * num // den, num, den)
        for offset in offsets[:1]:
            got[num, den, offset] = slice(base, base + wide)
            base += wide
    return got


def one_hot(wide, offset, num, den):
    shape = (wide, TILE)
    return (iota(shape, 1) * num // den + offset == iota(shape, 0)).astype(BF16)


def write_constants(picks_ref, expand_ref, block):
    rows = picks_ref.shape[0]
    parts = []
    for num, den in HARMONICS:
        shape = (rows, rows * num // den)
        parts.append((iota(shape, 0) * num // den == iota(shape, 1)).astype(BF16))
    picks_ref[...] = jnp.concatenate(parts, 1)
    for (num, den, offset), at in expands(block).items():
        expand_ref[at, :] = one_hot(at.stop - at.start, offset, num, den)


def stretch(plane, expand_ref, block, num, den):
    part_rows, part_cols = plane.shape
    starts, offsets, wide = stretch_plan(part_cols, num, den)
    done = {}
    for offset in offsets:
        members = [j for j, start in enumerate(starts) if start % LANES == offset]
        bases = [starts[j] - offset for j in members]
        stacked = jnp.concatenate([plane[:, base : base + wide] for base in bases], 0)
        at = expands(block).get((num, den, offset))
        matrix = one_hot(wide, offset, num, den) if at is None else expand_ref[at, :]
        spread = dot(stacked, matrix).astype(BF16)
        for k, j in enumerate(members):
            done[j] = spread[k * part_rows : (k + 1) * part_rows]
    return jnp.concatenate([done[j] for j in range(len(starts))], 1)


def group_order(owners):
    first = owners * 3 // 4 - 1
    return (first, *(j for j in range(owners) if j != first))


def bins(all_ref, unit, start, count):
    owners, _, block = all_ref.shape
    per = block // unit
    first = group_order(owners)[0]
    got = []
    for k in range(count):
        at = start + k
        inside = jnp.logical_and(at >= 0, at < owners * per)
        at = jnp.clip(at, 0, owners * per - 1)
        owner = at // per
        slot = jnp.where(owner == first, 0, jnp.where(owner < first, owner + 1, owner))
        column = pl.multiple_of((at - owner * per) * unit, LANES)
        piece = all_ref[slot, :, pl.ds(column, unit)].astype(F32)
        got.append(jnp.where(inside, piece, 0.0))
    return jnp.concatenate(got, 1)


def own_plane(w_ref, inner_ref, edge_ref, all_ref, side_ref, device, unit):
    count = w_ref.shape[0]
    half = count * LANES // 2
    width = half // unit
    here = device * (all_ref.shape[2] // unit)
    edges = []
    pad = jnp.zeros((2, 2 * LANES), F32)
    before = bins(all_ref, unit, here - width, width)
    hankel(jnp.concatenate([before, pad], 1), side_ref.at[0])
    after = bins(all_ref, unit, here + all_ref.shape[2] // unit, width)
    hankel(jnp.concatenate([pad, after, pad[:, :LANES]], 1), side_ref.at[1])
    for col in range(0, half, TILE):
        steps = [m for m in range(count) if col + m * LANES < half]
        edges.append(
            edge_ref[:, col : col + TILE]
            + dot(weights(w_ref, steps), hankel_tile(side_ref.at[0], col, steps))
        )
    shift = 2 * half - 2 * LANES
    for col in range(0, half, TILE):
        steps = [m for m in range(count) if col + m * LANES >= shift]
        edges.append(
            edge_ref[:, half + col : half + col + TILE]
            + dot(weights(w_ref, steps), hankel_tile(side_ref.at[1], col - shift, steps))
        )
    edges = [square(edge) for edge in edges]
    middle = len(edges) // 2
    return jnp.concatenate(edges[:middle] + [inner_ref[...]] + edges[middle:], 1)


def write_sum(own, pieces, picks_ref, out_ref, buffer_ref, sems):
    block = buffer_ref.shape[1]
    picks = picks_ref[...]
    chunks = sems.shape[0]
    width = block // chunks
    copies = []
    for n in range(chunks):
        at = slice(n * width, (n + 1) * width)
        rest = dot(picks, jnp.concatenate([piece[:, at] for piece in pieces], 0))
        buffer_ref[:, at] = own[:, at].astype(F32) + rest
        copy = pltpu.make_async_copy(buffer_ref.at[:, at], out_ref.at[:, at], sems.at[n])
        copy.start()
        copies.append(copy)
    for copy in copies:
        copy.wait()


def plane_kernel(
    w_ref, inner_ref, edge_ref, picks_ref, expand_ref, all_ref, out_ref, side_ref, buffer_ref, sems, *h_refs
):
    block = all_ref.shape[2]
    rows = w_ref.shape[1] // 3
    half = w_ref.shape[0] * LANES // 2
    device = lax.axis_index("freq")
    unit = math.gcd(half, *(block * num // den for num, den in HARMONICS))

    @pl.when(device > 0)
    def _():
        planes = [
            harmonic_plane(w_ref, all_ref, h_ref, device, unit, num, den)
            for (num, den), h_ref in zip(HARMONICS, h_refs)
        ]
        pieces = [
            stretch(plane, expand_ref, block, num, den)
            for plane, (num, den) in zip(planes, HARMONICS)
        ]
        own = own_plane(w_ref, inner_ref, edge_ref, all_ref, side_ref, device, unit)
        write_sum(own, pieces, picks_ref, out_ref, buffer_ref, sems)

    @pl.when(device == 0)
    def _():
        own = own_plane(w_ref, inner_ref, edge_ref, all_ref, side_ref, device, unit)
        pieces = [
            stretch(own[: rows * num // den, : block * num // den], expand_ref, block, num, den)
            for num, den in HARMONICS
        ]
        write_sum(own, pieces, picks_ref, out_ref, buffer_ref, sems)


def body(spectrum, template_bank, template_index):
    owners = lax.axis_size("freq")
    block = spectrum.shape[1]
    rows = template_index.shape[0]
    taps = template_bank.shape[2]
    half = taps // 2
    matrix_rows = max(at.stop for at in expands(block).values())
    hankels = [
        pltpu.VMEM((2 * LANES, block * num // den + taps - LANES), BF16) for num, den in HARMONICS
    ]
    mark = pl.pallas_call(
        first_kernel,
        out_shape=jax.ShapeDtypeStruct((8, LANES), F32),
        out_specs=VMEM,
        compiler_params=pltpu.CompilerParams(vmem_limit_bytes=1 << 20),
        cost_estimate=pl.CostEstimate(flops=4 * 10**9, bytes_accessed=16 << 20, transcendentals=0),
        name="first",
    )()
    shared, index = pl.pallas_call(
        share_kernel,
        out_shape=(
            jax.ShapeDtypeStruct((owners, 2, block), BF16),
            jax.ShapeDtypeStruct((1, rows), jnp.int32),
        ),
        in_specs=[ANY, VMEM, VMEM],
        out_specs=(VMEM,) * 2,
        compiler_params=pltpu.CompilerParams(vmem_limit_bytes=4 << 20),
        cost_estimate=pl.CostEstimate(flops=4 * 10**9, bytes_accessed=16 << 20, transcendentals=0),
        name="share",
    )(mark, spectrum, template_index.reshape(1, rows))
    everything = lax.all_to_all(
        shared,
        "freq",
        split_axis=0,
        concat_axis=0,
        tiled=True,
        axis_index_groups=[list(group_order(owners))],
    )
    w, inner, edge, picks, expand = pl.pallas_call(
        local_kernel,
        out_shape=(
            jax.ShapeDtypeStruct((taps // LANES, 3 * rows, LANES), BF16),
            jax.ShapeDtypeStruct((rows, block - 2 * half), BF16),
            jax.ShapeDtypeStruct((2 * rows, 2 * half), F32),
            jax.ShapeDtypeStruct((rows, sum(rows * num // den for num, den in HARMONICS)), BF16),
            jax.ShapeDtypeStruct((matrix_rows, TILE), BF16),
        ),
        in_specs=[VMEM] * 3,
        out_specs=(VMEM,) * 5,
        scratch_shapes=[pltpu.VMEM((2 * LANES, block + taps - LANES), BF16)],
        compiler_params=pltpu.CompilerParams(vmem_limit_bytes=24 << 20),
        name="local",
    )(index, template_bank, spectrum)
    return pl.pallas_call(
        plane_kernel,
        out_shape=jax.ShapeDtypeStruct((rows, block), F32),
        in_specs=[VMEM] * 6,
        out_specs=ANY,
        scratch_shapes=[
            pltpu.VMEM((2, 2 * LANES, half + TILE), BF16),
            pltpu.VMEM((rows, block), F32),
            pltpu.SemaphoreType.DMA((4,)),
        ]
        + hankels,
        compiler_params=pltpu.CompilerParams(vmem_limit_bytes=32 << 20),
        name="plane",
    )(w, inner, edge, picks, expand, everything)


def solution(mesh):
    return jax.shard_map(
        body,
        mesh=mesh,
        in_specs=(P(None, ("beam", "freq")), P(), P()),
        out_specs=P(None, ("beam", "freq")),
        check_vma=False,
    )
```

```python
import math

import jax
import jax.numpy as jnp
from jax import lax
from jax.experimental import pallas as pl
from jax.experimental.pallas import tpu as pltpu
from jax.sharding import PartitionSpec as P

LANES = 128
TILE = 256
HARMONICS = ((3, 4), (1, 2), (1, 4))
HELD = HARMONICS[:2]
F32 = jnp.float32
BF16 = jnp.bfloat16
VMEM = pl.BlockSpec(memory_space=pltpu.VMEM)
ANY = pl.BlockSpec(memory_space=pl.ANY)


def iota(shape, dim):
    return lax.broadcasted_iota(jnp.int32, shape, dim)


def dot(left, right):
    return jnp.dot(left, right, preferred_element_type=F32)


def square(pair):
    rows = pair.shape[0] // 2
    re, im = pair[:rows], pair[rows:]
    return (re * re + im * im).astype(BF16)


def hankel(window, h_ref):
    length = window.shape[1]
    kept = length - LANES
    for c in range(2):
        row = jnp.broadcast_to(window[c : c + 1, :], (8, length))
        for a in range(0, LANES // 8, 2):
            pair = [
                pltpu.roll(row, length - 8 * k - 7, 1, stride=1, stride_axis=0)[:, :kept]
                for k in (a, a + 1)
            ]
            at = c * LANES + 8 * a
            h_ref[at : at + 16, :kept] = jnp.concatenate(pair, 0).astype(BF16)


def hankel_tile(h_ref, col, steps, width=TILE):
    return jnp.concatenate(
        [h_ref[:, col + m * LANES : col + m * LANES + width] for m in steps], 0
    )


def half_step(w_ref, m, part, rows):
    all_rows = w_ref.shape[1] // 3
    picked = ((0, 2), (1, 0))[part]
    return jnp.concatenate([w_ref[m, k * all_rows : k * all_rows + rows, :] for k in picked], 1)


def weights(w_ref, steps):
    rows = w_ref.shape[1] // 3
    return jnp.concatenate(
        [
            jnp.concatenate([half_step(w_ref, m, part, rows) for part in (0, 1)], 0)
            for m in steps
        ],
        1,
    )


def first_kernel(mark_ref):
    mark_ref[...] = jnp.zeros(mark_ref.shape, F32)


def share_kernel(mark_ref, own_ref, index_ref, shared_ref, index_out_ref):
    for j in range(shared_ref.shape[0]):
        shared_ref[j] = own_ref[...]
    index_out_ref[...] = index_ref[...]


def local_kernel(
    index_ref, bank_ref, own_ref, w_ref, inner_ref, edge_ref, picks_ref, expand_ref, h_ref
):
    rows = index_ref.shape[1]
    bank = bank_ref.shape[1]
    taps = bank_ref.shape[2]
    half = taps // 2
    block = own_ref.shape[1]
    count = taps // LANES
    order = iota((LANES, LANES), 1)
    order = (order // 8) * 8 + 7 - order % 8
    flip = (iota((LANES, LANES), 0) == order).astype(BF16)
    zeros = jnp.zeros((2, half), F32)
    hankel(jnp.concatenate([zeros, own_ref[...].astype(F32), zeros], 1), h_ref)
    picked = (iota((bank, rows), 0) == index_ref[...]).astype(BF16)
    for m in range(count):
        part = []
        for c in range(2):
            chunk = bank_ref[c, :, m * LANES : (m + 1) * LANES]
            chunk = dot(chunk, flip).astype(BF16)
            part.append(
                lax.dot_general(
                    picked, chunk, (((0,), (0,)), ((), ())), preferred_element_type=F32
                )
            )
        re, im = part
        w_ref[m, :rows] = re.astype(BF16)
        w_ref[m, rows : 2 * rows] = im.astype(BF16)
        w_ref[m, 2 * rows :] = (-im).astype(BF16)
    write_constants(picks_ref, expand_ref, block)
    for col in range(0, block, TILE):
        steps = [
            m
            for m in range(count)
            if col + m * LANES + TILE + LANES - 1 > half and col + m * LANES < half + block
        ]
        got = dot(weights(w_ref, steps), hankel_tile(h_ref, col, steps))
        if half <= col < block - half:
            inner_ref[:, col - half : col - half + TILE] = square(got)
        else:
            at = col if col < half else col - block + 2 * half
            edge_ref[:, at : at + TILE] = got


def packed(w_ref, h_ref, rows, cols, pack):
    count = w_ref.shape[0]
    all_rows = w_ref.shape[1] // 3
    steps = range(0, count, pack)
    left = jnp.concatenate(
        [
            jnp.concatenate(
                [half_step(w_ref, m + k, part, rows) for k in range(pack) for part in (0, 1)],
                0,
            )
            for m in steps
        ],
        1,
    )
    if pack == 1:
        return jnp.concatenate(
            [square(dot(left, hankel_tile(h_ref, col, steps))) for col in range(0, cols, TILE)], 1
        )
    done = []
    for col in range(0, cols, TILE):
        got = dot(left, hankel_tile(h_ref, col, steps))
        high = got[2 * rows :]
        if col > 0:
            done.append(square(low + jnp.concatenate([rest, high[:, :LANES]], 1)))
        low, rest = got[: 2 * rows], high[:, LANES:]
    high = dot(left[2 * rows :], hankel_tile(h_ref, cols, steps, LANES))
    done.append(square(low + jnp.concatenate([rest, high], 1)))
    return jnp.concatenate(done, 1)


def harmonic_plane(w_ref, all_ref, h_ref, device, unit, num, den):
    count = w_ref.shape[0]
    rows = w_ref.shape[1] // 3
    taps = count * LANES
    part_rows, part_cols = rows * num // den, all_ref.shape[2] * num // den
    start = device * (part_cols // unit) - taps // 2 // unit
    hankel(bins(all_ref, unit, start, (part_cols + taps) // unit), h_ref)
    return packed(w_ref, h_ref, part_rows, part_cols, min(2, rows // part_rows))


def stretch_plan(part_cols, num, den):
    tiles = part_cols * den // num // TILE
    starts = [j * TILE * num // den for j in range(tiles)]
    offsets = sorted({start % LANES for start in starts})
    wide = -(-(max(offsets) + TILE * num // den) // LANES) * LANES
    return starts, offsets, wide


def expands(block):
    got = {}
    base = 0
    for num, den in HELD:
        _, offsets, wide = stretch_plan(block * num // den, num, den)
        for offset in offsets[:1]:
            got[num, den, offset] = slice(base, base + wide)
            base += wide
    return got


def one_hot(wide, offset, num, den):
    shape = (wide, TILE)
    return (iota(shape, 1) * num // den + offset == iota(shape, 0)).astype(BF16)


def write_constants(picks_ref, expand_ref, block):
    rows = picks_ref.shape[0]
    parts = []
    for num, den in HARMONICS:
        shape = (rows, rows * num // den)
        parts.append((iota(shape, 0) * num // den == iota(shape, 1)).astype(BF16))
    picks_ref[...] = jnp.concatenate(parts, 1)
    for (num, den, offset), at in expands(block).items():
        expand_ref[at, :] = one_hot(at.stop - at.start, offset, num, den)


def stretch(plane, expand_ref, block, num, den):
    part_rows, part_cols = plane.shape
    starts, offsets, wide = stretch_plan(part_cols, num, den)
    done = {}
    for offset in offsets:
        members = [j for j, start in enumerate(starts) if start % LANES == offset]
        bases = [starts[j] - offset for j in members]
        stacked = jnp.concatenate([plane[:, base : base + wide] for base in bases], 0)
        at = expands(block).get((num, den, offset))
        matrix = one_hot(wide, offset, num, den) if at is None else expand_ref[at, :]
        spread = dot(stacked, matrix).astype(BF16)
        for k, j in enumerate(members):
            done[j] = spread[k * part_rows : (k + 1) * part_rows]
    return jnp.concatenate([done[j] for j in range(len(starts))], 1)


def group_order(owners):
    first = owners * 3 // 4 - 1
    return (first, *(j for j in range(owners) if j != first))


def bins(all_ref, unit, start, count):
    owners, _, block = all_ref.shape
    per = block // unit
    first = group_order(owners)[0]
    got = []
    for k in range(count):
        at = start + k
        inside = jnp.logical_and(at >= 0, at < owners * per)
        at = jnp.clip(at, 0, owners * per - 1)
        owner = at // per
        slot = jnp.where(owner == first, 0, jnp.where(owner < first, owner + 1, owner))
        column = pl.multiple_of((at - owner * per) * unit, LANES)
        piece = all_ref[slot, :, pl.ds(column, unit)].astype(F32)
        got.append(jnp.where(inside, piece, 0.0))
    return jnp.concatenate(got, 1)


def own_plane(w_ref, inner_ref, edge_ref, all_ref, side_ref, device, unit):
    count = w_ref.shape[0]
    half = count * LANES // 2
    width = half // unit
    here = device * (all_ref.shape[2] // unit)
    edges = []
    pad = jnp.zeros((2, 2 * LANES), F32)
    before = bins(all_ref, unit, here - width, width)
    hankel(jnp.concatenate([before, pad], 1), side_ref.at[0])
    after = bins(all_ref, unit, here + all_ref.shape[2] // unit, width)
    hankel(jnp.concatenate([pad, after, pad[:, :LANES]], 1), side_ref.at[1])
    for col in range(0, half, TILE):
        steps = [m for m in range(count) if col + m * LANES < half]
        edges.append(
            edge_ref[:, col : col + TILE]
            + dot(weights(w_ref, steps), hankel_tile(side_ref.at[0], col, steps))
        )
    shift = 2 * half - 2 * LANES
    for col in range(0, half, TILE):
        steps = [m for m in range(count) if col + m * LANES >= shift]
        edges.append(
            edge_ref[:, half + col : half + col + TILE]
            + dot(weights(w_ref, steps), hankel_tile(side_ref.at[1], col - shift, steps))
        )
    edges = [square(edge) for edge in edges]
    middle = len(edges) // 2
    return jnp.concatenate(edges[:middle] + [inner_ref[...]] + edges[middle:], 1)


def write_sum(own, pieces, picks_ref, out_ref, buffer_ref, sems):
    block = buffer_ref.shape[1]
    picks = picks_ref[...]
    chunks = sems.shape[0]
    width = block // chunks
    copies = []
    for n in range(chunks):
        at = slice(n * width, (n + 1) * width)
        rest = dot(picks, jnp.concatenate([piece[:, at] for piece in pieces], 0))
        buffer_ref[:, at] = own[:, at].astype(F32) + rest
        copy = pltpu.make_async_copy(buffer_ref.at[:, at], out_ref.at[:, at], sems.at[n])
        copy.start()
        copies.append(copy)
    for copy in copies:
        copy.wait()


def plane_kernel(
    w_ref, inner_ref, edge_ref, picks_ref, expand_ref, all_ref, out_ref, side_ref, buffer_ref, sems, *h_refs
):
    block = all_ref.shape[2]
    rows = w_ref.shape[1] // 3
    half = w_ref.shape[0] * LANES // 2
    device = lax.axis_index("freq")
    unit = math.gcd(half, *(block * num // den for num, den in HARMONICS))

    @pl.when(device > 0)
    def _():
        planes = [
            harmonic_plane(w_ref, all_ref, h_ref, device, unit, num, den)
            for (num, den), h_ref in zip(HARMONICS, h_refs)
        ]
        pieces = [
            stretch(plane, expand_ref, block, num, den)
            for plane, (num, den) in zip(planes, HARMONICS)
        ]
        own = own_plane(w_ref, inner_ref, edge_ref, all_ref, side_ref, device, unit)
        write_sum(own, pieces, picks_ref, out_ref, buffer_ref, sems)

    @pl.when(device == 0)
    def _():
        own = own_plane(w_ref, inner_ref, edge_ref, all_ref, side_ref, device, unit)
        pieces = [
            stretch(own[: rows * num // den, : block * num // den], expand_ref, block, num, den)
            for num, den in HARMONICS
        ]
        write_sum(own, pieces, picks_ref, out_ref, buffer_ref, sems)


def body(spectrum, template_bank, template_index):
    owners = lax.axis_size("freq")
    block = spectrum.shape[1]
    rows = template_index.shape[0]
    taps = template_bank.shape[2]
    half = taps // 2
    matrix_rows = max(at.stop for at in expands(block).values())
    hankels = [
        pltpu.VMEM((2 * LANES, block * num // den + taps - LANES), BF16) for num, den in HARMONICS
    ]
    mark = pl.pallas_call(
        first_kernel,
        out_shape=jax.ShapeDtypeStruct((8, LANES), F32),
        out_specs=VMEM,
        compiler_params=pltpu.CompilerParams(vmem_limit_bytes=1 << 20),
        cost_estimate=pl.CostEstimate(flops=4 * 10**9, bytes_accessed=16 << 20, transcendentals=0),
        name="first",
    )()
    shared, index = pl.pallas_call(
        share_kernel,
        out_shape=(
            jax.ShapeDtypeStruct((owners, 2, block), BF16),
            jax.ShapeDtypeStruct((1, rows), jnp.int32),
        ),
        in_specs=[ANY, VMEM, VMEM],
        out_specs=(VMEM,) * 2,
        compiler_params=pltpu.CompilerParams(vmem_limit_bytes=4 << 20),
        cost_estimate=pl.CostEstimate(flops=4 * 10**9, bytes_accessed=16 << 20, transcendentals=0),
        name="share",
    )(mark, spectrum, template_index.reshape(1, rows))
    everything = lax.all_to_all(
        shared,
        "freq",
        split_axis=0,
        concat_axis=0,
        tiled=True,
        axis_index_groups=[list(group_order(owners))],
    )
    w, inner, edge, picks, expand = pl.pallas_call(
        local_kernel,
        out_shape=(
            jax.ShapeDtypeStruct((taps // LANES, 3 * rows, LANES), BF16),
            jax.ShapeDtypeStruct((rows, block - 2 * half), BF16),
            jax.ShapeDtypeStruct((2 * rows, 2 * half), F32),
            jax.ShapeDtypeStruct((rows, sum(rows * num // den for num, den in HARMONICS)), BF16),
            jax.ShapeDtypeStruct((matrix_rows, TILE), BF16),
        ),
        in_specs=[VMEM] * 3,
        out_specs=(VMEM,) * 5,
        scratch_shapes=[pltpu.VMEM((2 * LANES, block + taps - LANES), BF16)],
        compiler_params=pltpu.CompilerParams(vmem_limit_bytes=24 << 20),
        name="local",
    )(index, template_bank, spectrum)
    return pl.pallas_call(
        plane_kernel,
        out_shape=jax.ShapeDtypeStruct((rows, block), F32),
        in_specs=[VMEM] * 6,
        out_specs=ANY,
        scratch_shapes=[
            pltpu.VMEM((2, 2 * LANES, half + TILE), BF16),
            pltpu.VMEM((rows, block), F32),
            pltpu.SemaphoreType.DMA((4,)),
        ]
        + hankels,
        compiler_params=pltpu.CompilerParams(vmem_limit_bytes=32 << 20),
        name="plane",
    )(w, inner, edge, picks, expand, everything)


def solution(mesh):
    return jax.shard_map(
        body,
        mesh=mesh,
        in_specs=(P(None, ("beam", "freq")), P(), P()),
        out_specs=P(None, ("beam", "freq")),
        check_vma=False,
    )
```
